512 devices in a mesh: dp: 2 (over core), ctx: 32 (over x, y), exp: 8 (over z).
Axes of the slice: x: 4, y: 8, z: 8, core: 2. Of those that a mesh axis runs over, the one named last changes fastest.
Arguments:
- residual: bfloat16 [2, 4096, 2048], P('dp', 'ctx'), may hold values from -6 to 6
- queries: bfloat16 [2, 4096, 2, 1024], P('dp', 'ctx', None, 'exp'), may hold values from -20 to 20
- keys: bfloat16 [2, 4096, 1024], P('dp', 'ctx', 'exp'), may hold values from -20 to 20
- values: bfloat16 [2, 4096, 1024], P('dp', 'ctx', 'exp'), may hold values from -6 to 6
- attn_routes: int32 [2, 4096, 2], P('dp', 'ctx'), may hold values from 0 to 7, all different within a row; in each aligned block of 128 rows (0 to 127, 128 to 255, ..., all dimensions but the last counted through in order) at most 40 rows name the same one
- attn_gates: float32 [2, 4096, 2], P('dp', 'ctx'), may hold values from 0.3 to 1
- out_weight: bfloat16 [8, 1024, 2048], P('exp', None, 'ctx'), may hold values from -0.75 to 0.75
- norm_gain: float32 [2048], replicated, may hold values from 0.5 to 1.5
- ffn_routes: int32 [2, 4096, 2], P('dp', 'ctx'), may hold values from 0 to 7, all different within a row; in each aligned block of 128 rows (0 to 127, 128 to 255, ..., all dimensions but the last counted through in order) at most 32 rows name the same one
- ffn_gates: float32 [2, 4096, 2], P('dp', 'ctx'), may hold values from 0.3 to 1
- w_gate: bfloat16 [8, 2048, 5632], P('exp', None, 'ctx'), may hold values from -0.125 to 0.125
- w_up: bfloat16 [8, 2048, 5632], P('exp', None, 'ctx'), may hold values from -0.125 to 0.125
- w_down: bfloat16 [8, 5632, 2048], P('exp', 'ctx'), may hold values from -0.15625 to 0.15625
Outputs:
- layer_out: bfloat16 [2, 4096, 2048], P('dp', 'ctx')
The draws below stay inside these ranges and needn't reach their ends.
Inputs may be any that keep to these rules, and one draw needn't show every extreme that they name: `attn_routes`: no attention expert is named by more than 40 of the rows of one device; a row's two experts differ. `ffn_routes`: every FFN expert is named by exactly 32 of the rows of one device; a row's two experts differ.
All inputs are finite; a program needn't handle non-finite values.
Results may differ from the reference program's by a relative error of at most 0.02.
Values may be sent and summed in bfloat16 or wider, within the bound.
A program may use at most 64 MiB of HBM per device.

```python
import math
import jax
import jax.numpy as jnp
import numpy as np
from jax import lax

D = 2048
FF = 5632
HEAD = 128
HEADS = 8
TOK_DEV = 128
EXPERTS = 8
SEQS = 2
SEQ_LEN = 4096
ATTN_CAP = 40
FFN_CAP = 32
N_CTX = 32


def shared_rows(key):
    return jnp.clip(jax.random.normal(key, (SEQS, SEQ_LEN, HEADS * HEAD), jnp.float32), -4.0, 4.0)


def draw_keys(key, part):
    common = shared_rows(key)
    key = jax.random.fold_in(key, 3)
    return jnp.clip(jax.random.normal(key, common.shape, jnp.float32), -4.0, 4.0).astype(jnp.bfloat16)


def draw_queries(key, part):
    key = jax.random.fold_in(key, 5)
    query_shape = (SEQS, SEQ_LEN, 2, HEADS * HEAD)
    return jnp.clip(jax.random.normal(key, query_shape, jnp.float32), -4.0, 4.0).astype(jnp.bfloat16)


def levels(rng, dims, shards, low, high):
    loudness = 1.0
    for dim, shards_of in shards:
        steps = jax.random.uniform(jax.random.fold_in(jax.random.fold_in(rng, 6), dim), (shards_of,), jnp.float32, low / len(shards), high / len(shards))
        loudness = loudness * jnp.repeat(jnp.exp(steps), dims[dim] // shards_of).reshape((-1,) + (1,) * (len(dims) - 1 - dim))
    return loudness


def routed_block(own_key, own, number, rows, number_of, top, most, slope):
    order = jax.random.permutation(own_key, number_of)
    crowded, usual = load_shares(number_of, rows * top, most, slope, True), load_shares(number_of, rows * top, most, slope, False)
    places = jnp.arange(number_of)

    def named(sizes, rotation):
        used = int((sizes > 0).sum())
        fixed = max(1, used // 4)
        passed = fixed + (places - fixed + rotation * (used - fixed)) % max(1, number_of - fixed)
        return jnp.zeros((number_of,), jnp.int32).at[order[jnp.where(places < fixed, places, passed)]].set(jnp.asarray(sizes, jnp.int32))

    sizes = jnp.where(number % 4 == 0, named(crowded, number // 4), named(usual, number - number // 4 - 1))
    mixed = jax.random.permutation(jax.random.fold_in(own, 3), number_of)
    source_of, receiver = mixed[0:number_of // 2 * 2:2], mixed[1:number_of // 2 * 2:2]
    slack = jnp.minimum(sizes[source_of] - 1, most - sizes[receiver]) // 2
    slack = jnp.where((source_of == order[0]) | (receiver == order[0]) | (sizes[receiver] == 0), 0, jnp.maximum(slack, 0))
    passed = jax.random.randint(jax.random.fold_in(own, 4), (number_of // 2,), 0, 1 << 20) % (slack + 1)
    sizes = sizes.at[source_of].add(-passed).at[receiver].add(passed)
    labels = jnp.searchsorted(jnp.cumsum(sizes), jnp.arange(rows * top), side="right").astype(jnp.int32)
    table = labels.reshape(top, rows).T
    table = table[jax.random.permutation(jax.random.fold_in(own, 1), rows)]
    rotation = jax.random.randint(jax.random.fold_in(own, 2), (rows, 1), 0, top)
    return jnp.take_along_axis(table, (jnp.arange(top)[None, :] + rotation) % top, axis=1)


def load_shares(number_of, total, most, skew, full):
    portions = [(1 << 20) // math.isqrt(rank ** skew) + 1 for rank in range(1, number_of + 1)]
    largest = most if full else min(most, max(-(-total // number_of), total * portions[0] // sum(portions)))
    least = 1 if total - largest >= number_of - 1 else 0
    holding, rest = [largest] + [least] * (number_of - 1), total - largest - least * (number_of - 1)
    while rest > 0:
        free = [i for i in range(1, number_of) if holding[i] < largest] or [i for i in range(1, number_of) if holding[i] < most]
        whole, remaining = sum([portions[i] for i in free]), rest
        for i in free:
            addition = min(most - holding[i], max(1, remaining * portions[i] // whole), rest)
            holding[i] = holding[i] + addition
            rest = rest - addition
    return np.array(holding)


def centred(key, shape, deviation, reach, split=(), held_as=jnp.bfloat16):
    drawn = jax.random.normal(key, shape, jnp.float32) * deviation
    if len(split) > 0:
        drawn = levels(key, shape, split, -0.22, 0.18) * drawn
    return jnp.clip(drawn, min=-reach, max=reach).astype(held_as)


def setup_inputs(seed: int = 0) -> dict:
    seeds = jax.random.split(jax.random.key(seed), 14)
    residual = centred(seeds[0], (SEQS, SEQ_LEN, D), 1.0, 6.0, ((0, 2), (1, 32)))
    queries = draw_queries(jax.random.fold_in(seeds[13], 71), 0)
    keys = draw_keys(jax.random.fold_in(seeds[13], 71), 0)
    values = centred(seeds[3], (SEQS, SEQ_LEN, HEADS * HEAD), 1.0, 6.0, ((0, 2), (1, 32), (2, 8)))
    attn_routes_keys = jax.random.split(jax.random.fold_in(seeds[4], 1), SEQS * SEQ_LEN // TOK_DEV)
    attn_routes_turns = jax.random.permutation(jax.random.fold_in(seeds[4], 3), SEQS * SEQ_LEN // TOK_DEV)
    attn_routes = jax.vmap(lambda own, number: routed_block(jax.random.fold_in(seeds[4], 2), own, number, TOK_DEV, EXPERTS, 2, ATTN_CAP, 2))(attn_routes_keys, attn_routes_turns).reshape((SEQS, SEQ_LEN, 2))
    attn_gates = jnp.clip(0.3 + 0.7 * jax.random.uniform(seeds[5], (SEQS, SEQ_LEN, 2), jnp.float32) ** levels(seeds[5], (SEQS, SEQ_LEN, 2), ((0, 2), (1, 32)), -0.2, 0.2), 0.3, 1.0)
    out_weight = centred(seeds[6], (EXPERTS, HEADS * HEAD, D), (HEADS * HEAD // 16) ** -0.5, 0.75, ((0, 8), (2, 32)))
    norm_gain = jnp.clip(1.0 + 0.1 * jax.random.normal(seeds[7], (D,), jnp.float32), 0.5, 1.5)
    ffn_routes_keys = jax.random.split(jax.random.fold_in(seeds[8], 1), SEQS * SEQ_LEN // TOK_DEV)
    ffn_routes_turns = jax.random.permutation(jax.random.fold_in(seeds[8], 3), SEQS * SEQ_LEN // TOK_DEV)
    ffn_routes = jax.vmap(lambda own, number: routed_block(jax.random.fold_in(seeds[8], 2), own, number, TOK_DEV, EXPERTS, 2, FFN_CAP, 0))(ffn_routes_keys, ffn_routes_turns).reshape((SEQS, SEQ_LEN, 2))
    ffn_gates = jnp.clip(0.3 + 0.7 * jax.random.uniform(seeds[9], (SEQS, SEQ_LEN, 2), jnp.float32) ** levels(seeds[9], (SEQS, SEQ_LEN, 2), ((0, 2), (1, 32)), -0.2, 0.2), 0.3, 1.0)
    w_gate = centred(seeds[10], (EXPERTS, D, FF), D ** -0.5, 0.125, ((0, 8), (2, 32)))
    w_up = centred(seeds[11], (EXPERTS, D, FF), D ** -0.5, 0.125, ((0, 8), (2, 32)))
    w_down = centred(seeds[12], (EXPERTS, FF, D), (FF // 4) ** -0.5, 0.15625, ((0, 8), (1, 32)))
    return dict(residual=residual, queries=queries, keys=keys, values=values, attn_routes=attn_routes, attn_gates=attn_gates, out_weight=out_weight, norm_gain=norm_gain, ffn_routes=ffn_routes, ffn_gates=ffn_gates, w_gate=w_gate, w_up=w_up, w_down=w_down)


def rms_norm(stream_rows, gain_vector):
    mean_square = lax.optimization_barrier(jnp.mean(stream_rows * stream_rows, axis=-1, keepdims=True))
    return (stream_rows * lax.rsqrt(mean_square + 1e-06) * gain_vector).astype(jnp.bfloat16)

def attend_head(head_triple):
    query_rows, key_rows, value_rows = head_triple
    score_scale = 1.0 / math.sqrt(HEAD)
    scores = jnp.dot(query_rows, key_rows.T, preferred_element_type=jnp.float32) * score_scale
    query_pos = jnp.arange(SEQ_LEN * 2, dtype=jnp.int32) // 2
    key_pos = jnp.arange(SEQ_LEN, dtype=jnp.int32)
    allowed = key_pos[None, :] <= query_pos[:, None]
    row_max = lax.optimization_barrier(jnp.max(jnp.where(allowed, scores, -jnp.inf), axis=1, keepdims=True))
    weights = jnp.where(allowed, jnp.exp(scores - row_max), 0.0)
    row_total = lax.optimization_barrier(jnp.sum(weights, axis=1, keepdims=True))
    summed = jnp.dot(weights.astype(jnp.bfloat16), value_rows, preferred_element_type=jnp.float32)
    return (summed / row_total).astype(jnp.bfloat16)

def reference(residual, queries, keys, values, attn_routes, attn_gates, out_weight, norm_gain, ffn_routes, ffn_gates, w_gate, w_up, w_down):
    head_queries = queries.reshape(SEQS, SEQ_LEN, 2, HEADS, HEAD).transpose(0, 3, 1, 2, 4).reshape(SEQS * HEADS, SEQ_LEN * 2, HEAD)
    head_keys = keys.reshape(SEQS, SEQ_LEN, HEADS, HEAD).transpose(0, 2, 1, 3).reshape(SEQS * HEADS, SEQ_LEN, HEAD)
    head_values = values.reshape(SEQS, SEQ_LEN, HEADS, HEAD).transpose(0, 2, 1, 3).reshape(SEQS * HEADS, SEQ_LEN, HEAD)
    attended = lax.map(attend_head, (head_queries, head_keys, head_values))
    attended = attended.reshape(SEQS, HEADS, SEQ_LEN, 2, HEAD).transpose(0, 2, 3, 1, 4).reshape(SEQS * SEQ_LEN * 2, HEADS * HEAD)
    slot_total = SEQS * SEQ_LEN * 2
    attn_flat = attn_routes.reshape(slot_total)
    bound = SEQS * N_CTX * ATTN_CAP
    projected = jnp.zeros((slot_total, D), jnp.bfloat16)
    for expert in range(EXPERTS):
        chosen = attn_flat == expert
        positions = jnp.nonzero(chosen, size=bound, fill_value=0)[0].astype(jnp.int32)
        in_range = jnp.arange(bound, dtype=jnp.int32) < jnp.sum(chosen.astype(jnp.int32))
        rows_out = jnp.dot(attended[positions], out_weight[expert], preferred_element_type=jnp.float32).astype(jnp.bfloat16)
        targets = jnp.where(in_range, positions, slot_total).astype(jnp.int32)
        projected = projected.at[targets].set(rows_out, mode='drop')
    attn_out = lax.optimization_barrier(jnp.sum(projected.astype(jnp.float32).reshape(SEQS, SEQ_LEN, 2, D) * attn_gates[..., None], axis=2))
    resid = residual.astype(jnp.float32) + attn_out
    normed = rms_norm(resid, norm_gain)
    ffn_flat = ffn_routes.reshape(slot_total)
    normed_flat = normed.reshape(SEQS * SEQ_LEN, D)
    per_expert = SEQS * N_CTX * FFN_CAP
    unit_block = FF // N_CTX
    expert_out = jnp.zeros((slot_total, D), jnp.float32)
    for expert in range(EXPERTS):
        positions = jnp.nonzero(ffn_flat == expert, size=per_expert, fill_value=0)[0].astype(jnp.int32)
        expert_in = normed_flat[positions // 2]
        gate_proj = jnp.dot(expert_in, w_gate[expert], preferred_element_type=jnp.float32)
        up_proj = jnp.dot(expert_in, w_up[expert], preferred_element_type=jnp.float32)
        hidden = (jax.nn.silu(gate_proj) * up_proj).astype(jnp.bfloat16)
        hidden_blocks = hidden.reshape(per_expert, N_CTX, unit_block).transpose(1, 0, 2)
        down_blocks = w_down[expert].reshape(N_CTX, unit_block, D)

        def add_block(running, operands):
            block_term = jnp.dot(operands[0], operands[1], preferred_element_type=jnp.float32).astype(jnp.bfloat16)
            block_term = lax.optimization_barrier(block_term)
            return (running + block_term.astype(jnp.float32), None)
        summed, unused = lax.scan(add_block, jnp.zeros((per_expert, D), jnp.float32), (hidden_blocks, down_blocks))
        expert_out = expert_out.at[positions].set(summed)
    ffn_total = lax.optimization_barrier(jnp.sum(expert_out.reshape(SEQS, SEQ_LEN, 2, D) * ffn_gates[..., None], axis=2))
    return (resid + ffn_total).astype(jnp.bfloat16)
```

```python
import functools
import math

import jax
import jax.numpy as jnp
from jax import lax
from jax.experimental import pallas as pl
from jax.experimental.pallas import tpu as pltpu
from jax.sharding import PartitionSpec as P

MESH = pl.DeviceIdType.MESH
BF = jnp.bfloat16
F32 = jnp.float32
NX, NY, NZ = 4, 8, 8
TOK = 128
D = 2048
HEAD = 128
ACAP = 48
FCAP = 32
NEG = -1e30


def nt(a, b):
    return lax.dot_general(a, b, (((1,), (1,)), ((), ())), preferred_element_type=F32)


def tn(a, b):
    return lax.dot_general(a, b, (((0,), (0,)), ((), ())), preferred_element_type=F32)


def nn(a, b):
    return jnp.dot(a, b, preferred_element_type=F32)


def wrap(v, n):
    return lax.rem(v + 2 * n, n)


class Copies:
    def __init__(self):
        self.sent = []

    def send(self, src, dst, ssem, rsem, dev):
        cp = pltpu.make_async_remote_copy(
            src_ref=src, dst_ref=dst, send_sem=ssem, recv_sem=rsem, device_id=dev, device_id_type=MESH
        )
        cp.start()
        self.sent.append(cp)
        return cp

    def drain(self):
        for cp in self.sent:
            cp.wait_send()


class Ring:
    def __init__(self, copies, at, pos, right, left, ssem, rsem, chunks):
        self.copies, self.at, self.pos = copies, at, pos
        self.devs = (right, left)
        self.ssem, self.rsem, self.chunks = ssem, rsem, chunks
        self.cps = {}

    def carries(self, way, step, j):
        return step < 4 or (j < self.chunks // 2) == (way == 0)

    def slot(self, way, step):
        return wrap(self.pos - step if way == 0 else self.pos + step, 8)

    def start(self, step, j, own=None):
        for way in (0, 1):
            if self.carries(way, step, j):
                slot = self.slot(way, step - 1)
                src = self.at(slot, j) if own is None else own(j)
                self.cps[way, step, j] = self.copies.send(
                    src, self.at(slot, j), self.ssem.at[way, step - 1, j], self.rsem.at[way, step - 1, j], self.devs[way]
                )

    def wait(self, step, j):
        for way in (0, 1):
            if self.carries(way, step, j):
                self.cps[way, step, j].wait_recv()

    def forward(self, step, own=None):
        for j in range(self.chunks):
            if step > 1:
                self.wait(step - 1, j)
            self.start(step, j, own if step == 1 else None)

    def finish(self):
        for j in range(self.chunks):
            self.wait(4, j)


def layer_kernel(
    meta, res, q, kv, gain, wo, gu, wd, out,
    KV, QB, OB, SB, OS, SS, WO, GU, WD, PK, ER, PR, MG, FG, XN, YP, RR, RL, EO, RES,
    bsem, kv_s, kv_r, q_s, q_r, o_s, o_r, wx_s, wx_r, wy_s, wy_r, wc_s, wc_r,
    fx_s, fx_r, fc_s, fc_r, a_s, a_r, p_s, p_r, x_s, x_r, y_s, y_r, e_s, e_r,
):
    j = lax.axis_index("dp")
    c = lax.axis_index("ctx")
    z = lax.axis_index("exp")
    x = c // NY
    y = c % NY
    cop = Copies()

    def xdev(k):
        return (j, wrap(x + k, NX) * NY + y, z)

    def ydev(k):
        return (j, x * NY + wrap(y + k, NY), z)

    def zdev(k):
        return (j, c, wrap(z + k, NZ))

    sib = (1 - j, c, z)
    half = lambda n, i: pl.ds(pl.multiple_of(i * n, n), n)

    for d in range(1, NX):
        OB[d] = jnp.zeros((HEAD, 2 * TOK), BF)
        SB[d] = jnp.concatenate(
            [jnp.full((1, 2 * TOK), NEG, F32), jnp.zeros((7, 2 * TOK), F32)], axis=0
        )

    barrier = pltpu.get_barrier_semaphore()
    partners = [xdev(k) for k in (1, 2, 3)] + [ydev(1), ydev(-1)] + [zdev(k) for k in range(1, 8)] + [sib]
    for dev in partners:
        pl.semaphore_signal(barrier, inc=1, device_id=dev, device_id_type=MESH)
    pl.semaphore_wait(barrier, len(partners))

    kvring = Ring(
        cop, lambda slot, k: KV.at[slot, k], y, ydev(1), ydev(-1), kv_s, kv_r, 2
    )
    kvring.forward(1, own=lambda k: kv.at[k])

    for d in range(1, NX):

        @pl.when(x >= d)
        def _():
            pltpu.make_async_remote_copy(
                src_ref=q, dst_ref=QB.at[d], send_sem=q_s.at[d], recv_sem=q_r.at[d],
                device_id=xdev(-d), device_id_type=MESH,
            ).start()

    own_w = [
        pltpu.make_async_copy(wo.at[half(256, j)], WO.at[x, y, half(256, j)], bsem.at[0]),
        pltpu.make_async_copy(gu, GU.at[x], bsem.at[1]),
        pltpu.make_async_copy(wd, WD.at[x], bsem.at[2]),
    ]
    for cp in own_w:
        cp.start()
    wx = [
        cop.send(
            wo.at[half(256, j)], WO.at[x, y, half(256, j)], wx_s.at[d - 1], wx_r.at[d - 1], xdev(d)
        )
        for d in (1, 2, 3)
    ]

    grow = half(1024, j)
    fx = []
    for way, step in ((0, 1), (1, -1)):
        fx.append(cop.send(gu.at[grow], GU.at[x, grow], fx_s.at[way, 0], fx_r.at[way, 0], xdev(step)))
        fx.append(
            cop.send(wd.at[:, grow], WD.at[x, :, grow], fx_s.at[way, 1], fx_r.at[way, 1], xdev(step))
        )

    KV[y] = kv[...]

    ar = jnp.concatenate([meta[0:1, :], meta[1:2, :]], axis=1)
    fr = jnp.concatenate([meta[4:5, :], meta[5:6, :]], axis=1)
    upper = (
        lax.broadcasted_iota(jnp.int32, (256, 256), 0) < lax.broadcasted_iota(jnp.int32, (256, 256), 1)
    ).astype(F32).astype(BF)

    def slots(route, cap):
        eid = lax.broadcasted_iota(jnp.int32, (8, 256), 0).astype(F32)
        onehot = (eid == route).astype(F32)
        before = nn(onehot.astype(BF), upper)
        return route * cap + jnp.sum(before * onehot, axis=0, keepdims=True)

    def iota0(rows, cols):
        return lax.broadcasted_iota(jnp.int32, (rows, cols), 0).astype(F32)

    aslot = slots(ar, ACAP)
    fslot = slots(fr, FCAP)
    disp = (iota0(8 * ACAP, 256) == aslot).astype(F32).astype(BF)

    def gate_table(slot, g0, g1, rows):
        rid = iota0(rows, TOK)
        t = jnp.where(rid == slot[:, :TOK], g0, 0.0) + jnp.where(rid == slot[:, TOK:], g1, 0.0)
        t = t.T
        hi = t.astype(BF)
        return hi, (t - hi.astype(F32)).astype(BF)

    mhi, mlo = gate_table(aslot, meta[2:3, :], meta[3:4, :], 8 * ACAP)
    MG[0] = mhi
    MG[1] = mlo
    fhi, flo = gate_table(fslot, meta[6:7, :], meta[7:8, :], 8 * FCAP)
    FG[0] = fhi
    FG[1] = flo
    mine = iota0(FCAP, TOK) + (z * FCAP).astype(F32)
    sel = (
        (mine == fslot[:, :TOK]).astype(F32) + (mine == fslot[:, TOK:]).astype(F32)
    ).astype(BF)

    kvring.forward(2)

    for cp in wx:
        cp.wait_recv()
    own_w[0].wait()
    wring = Ring(
        cop,
        lambda slot, k: WO.at[pl.ds(2 * k, 2), slot, half(256, j)],
        y, ydev(1), ydev(-1), wy_s, wy_r, 2,
    )
    wcs = []

    def to_sibling(n, slot):
        wcs.append(
            cop.send(
                WO.at[:, slot, half(256, j)], WO.at[:, slot, half(256, j)], wc_s.at[n], wc_r.at[n], sib
            )
        )

    kvring.forward(3)
    wring.forward(1)
    to_sibling(0, y)
    kvring.forward(4)
    kvring.finish()

    scale = 1.0 / math.sqrt(HEAD)
    keys = KV[:, 0].reshape(NY * TOK, HEAD)
    vals = KV[:, 1].reshape(NY * TOK, HEAD)

    def attend(queries, masked):
        s = nt(keys, queries) * scale
        if masked:
            kpos = lax.broadcasted_iota(jnp.int32, (NY * TOK, 2 * TOK), 0)
            lane = lax.broadcasted_iota(jnp.int32, (NY * TOK, 2 * TOK), 1)
            qpos = y * TOK + jnp.bitwise_and(lane, TOK - 1)
            s = jnp.where(kpos <= qpos, s, NEG)
        m = jnp.max(s, axis=0, keepdims=True)
        p = jnp.exp(s - m)
        l = jnp.sum(p, axis=0, keepdims=True)
        return tn(vals, p.astype(BF)), m, l

    for d in range(1, NX):

        @pl.when(x + d < NX)
        def _():
            pltpu.make_async_remote_copy(
                src_ref=q, dst_ref=QB.at[d], send_sem=q_s.at[d], recv_sem=q_r.at[d],
                device_id=xdev(-d), device_id_type=MESH,
            ).wait_recv()
            o, m, l = attend(QB[d], False)
            OS[d] = o.astype(BF)
            SS[d] = jnp.concatenate([m, l, jnp.zeros((6, 2 * TOK), F32)], axis=0)
            for src, dst, i in ((OS, OB, 0), (SS, SB, 1)):
                pltpu.make_async_remote_copy(
                    src_ref=src.at[d], dst_ref=dst.at[d], send_sem=o_s.at[d, i], recv_sem=o_r.at[d, i],
                    device_id=xdev(d), device_id_type=MESH,
                ).start()

    o, m, l = attend(q[...], True)

    wring.forward(2)
    to_sibling(1, wrap(y - 1, NY))
    to_sibling(2, wrap(y + 1, NY))

    for d in range(1, NX):

        @pl.when(x >= d)
        def _():
            for src, dst, i in ((OS, OB, 0), (SS, SB, 1)):
                pltpu.make_async_remote_copy(
                    src_ref=src.at[d], dst_ref=dst.at[d], send_sem=o_s.at[d, i], recv_sem=o_r.at[d, i],
                    device_id=xdev(d), device_id_type=MESH,
                ).wait_recv()

    top = m
    for d in range(1, NX):
        top = jnp.maximum(top, SB[d, 0:1, :])
    f = jnp.exp(m - top)
    o = o * f
    l = l * f
    for d in range(1, NX):
        f = jnp.exp(SB[d, 0:1, :] - top)
        o = o + OB[d].astype(F32) * f
        l = l + SB[d, 1:2, :] * f
    attended = (o / l).astype(BF)

    packed = nt(disp, attended).astype(BF)
    PK[...] = packed.reshape(NZ, ACAP, HEAD)
    acps = []
    for k in range(1, NZ):
        acps.append(
            cop.send(PK.at[wrap(z + k, NZ)], ER.at[z], a_s.at[k], a_r.at[k], zdev(k))
        )
    ER[z] = PK[z]

    wring.forward(3)
    to_sibling(3, wrap(y - 2, NY))
    to_sibling(4, wrap(y + 2, NY))

    for cp in fx:
        cp.wait_recv()
    ahead = []
    for way, step, base in ((0, 1, 0), (1, -1, 512)):
        rows = pl.ds(pl.multiple_of(j * 1024 + base, 512), 512)
        slot = wrap(x - step, NX)
        ahead.append(
            cop.send(GU.at[slot, rows], GU.at[slot, rows], fx_s.at[way, 2], fx_r.at[way, 2], xdev(step))
        )
        ahead.append(
            cop.send(
                WD.at[slot, :, rows], WD.at[slot, :, rows], fx_s.at[way, 3], fx_r.at[way, 3], xdev(step)
            )
        )
    fcs = []

    def weights_to_sibling(n, slot):
        fcs.append(cop.send(GU.at[slot, grow], GU.at[slot, grow], fc_s.at[n, 0], fc_r.at[n, 0], sib))
        fcs.append(
            cop.send(WD.at[slot, :, grow], WD.at[slot, :, grow], fc_s.at[n, 1], fc_r.at[n, 1], sib)
        )

    weights_to_sibling(0, wrap(x - 1, NX))
    weights_to_sibling(1, wrap(x + 1, NX))

    wring.forward(4)
    to_sibling(5, wrap(y - 3, NY))
    to_sibling(6, wrap(y + 3, NY))
    wring.finish()
    to_sibling(7, wrap(y + 4, NY))

    for cp in acps:
        cp.wait_recv()
    lhs = jnp.concatenate(
        [
            jnp.concatenate([ER[h] for h in range(4)], axis=1),
            jnp.concatenate([ER[h] for h in range(4, 8)], axis=1),
        ],
        axis=0,
    )
    for cp in wcs:
        cp.wait_recv()
    low = lax.broadcasted_iota(jnp.int32, (ACAP, HEAD), 1) < 64
    for i in range(NX * NY // 2):
        a, b = 2 * i, 2 * i + 1
        w = jnp.concatenate([WO[a // NY, a % NY], WO[b // NY, b % NY]], axis=1)
        r = nn(lhs, w)
        ra0, ra1 = r[:ACAP, :HEAD], r[ACAP:, :HEAD]
        rb0, rb1 = r[:ACAP, HEAD:], r[ACAP:, HEAD:]
        first = ra0 + pltpu.roll(ra1, 64, 1)
        second = pltpu.roll(rb0, 64, 1) + rb1
        PR[z, :, i * HEAD:(i + 1) * HEAD] = jnp.where(low, first, second).astype(BF)

    pring = Ring(
        cop, lambda slot, k: PR.at[slot, :, k * 512:(k + 1) * 512], z, zdev(1), zdev(-1), p_s, p_r, 4
    )
    for step in (1, 2, 3, 4):
        pring.forward(step)
    pring.finish()

    rows_all = PR[...].reshape(NZ * ACAP, D)
    own_hi = nn(sel, MG[0]).astype(BF)
    own_lo = nn(sel, MG[1]).astype(BF)
    own = nn(sel, res[...]) + nn(own_hi, rows_all) + nn(own_lo, rows_all)
    ms = jnp.mean(own * own, axis=1, keepdims=True)
    XN[y] = (own * lax.rsqrt(ms + 1e-6) * gain[...]).astype(BF)

    xring = Ring(
        cop, lambda slot, k: XN.at[slot, :, k * 512:(k + 1) * 512], y, ydev(1), ydev(-1), x_s, x_r, 4
    )
    xring.forward(1)
    RES[...] = res[...].astype(F32) + nn(MG[0], rows_all) + nn(MG[1], rows_all)
    xring.forward(2)
    for cp in ahead:
        cp.wait_recv()
    weights_to_sibling(2, wrap(x + 2, NX))
    xring.forward(3)
    xring.forward(4)
    xring.finish()
    own_w[1].wait()
    own_w[2].wait()
    for cp in fcs:
        cp.wait_recv()

    rows = XN[...].reshape(NY * FCAP, D)
    wide = []
    tails = []
    for i in range(2):
        a, b = 2 * i, 2 * i + 1
        g = nn(rows, jnp.concatenate([GU[a, :, 0:128], GU[b, :, 0:128]], axis=1))
        u = nn(rows, jnp.concatenate([GU[a, :, 256:384], GU[b, :, 256:384]], axis=1))
        t = nn(rows, jnp.concatenate([GU[a, :, 128:256], GU[b, :, 128:256]], axis=1))
        wide.append((g / (1.0 + jnp.exp(-g)) * u).astype(BF))
        for k in range(2):
            tk = t[:, k * 128:(k + 1) * 128]
            tails.append(tk / (1.0 + jnp.exp(-tk)) * pltpu.roll(tk, 64, 1))
    lowr = lax.broadcasted_iota(jnp.int32, (NY * FCAP, HEAD), 1) < 64
    tail = jnp.concatenate(
        [
            jnp.where(lowr, tails[0], pltpu.roll(tails[1], 64, 1)),
            jnp.where(lowr, tails[2], pltpu.roll(tails[3], 64, 1)),
        ],
        axis=1,
    ).astype(BF)
    hidden = jnp.concatenate([wide[0], wide[1], tail], axis=1)
    pad = jnp.zeros((16, 512), BF)
    for n in range(4):
        cols = slice(n * 512, (n + 1) * 512)
        w = jnp.concatenate(
            [WD[k, 0:128, cols] for k in range(4)]
            + [v for k in range(4) for v in (WD[k, 128:176, cols], pad)],
            axis=0,
        )
        YP[:, :, cols] = nn(hidden, w).astype(BF).reshape(NY, FCAP, 512)

    rcp, lcp = {}, {}
    for step in (1, 2, 3, 4):
        rd, ld = wrap(y + 5 - step, NY), wrap(y - 5 + step, NY)
        if step == 2:
            rcp[1].wait_recv()
            YP[rd, :, 0:1024] = (YP[rd, :, 0:1024].astype(F32) + RR[0, :, 0:1024].astype(F32)).astype(BF)
            lcp[1].wait_recv()
            YP[ld, :, 1024:2048] = (
                YP[ld, :, 1024:2048].astype(F32) + RL[0, :, 1024:2048].astype(F32)
            ).astype(BF)
        elif step > 2:
            rcp[step - 1].wait_recv()
            YP[rd] = (YP[rd].astype(F32) + RR[step - 2].astype(F32)).astype(BF)
            lcp[step - 1].wait_recv()
            YP[ld] = (YP[ld].astype(F32) + RL[step - 2].astype(F32)).astype(BF)
        if step == 1:
            rs, rt = YP.at[rd, :, 0:1024], RR.at[0, :, 0:1024]
            ls, lt = YP.at[ld, :, 1024:2048], RL.at[0, :, 1024:2048]
        else:
            rs, rt = YP.at[rd], RR.at[step - 1]
            ls, lt = YP.at[ld], RL.at[step - 1]
        rcp[step] = cop.send(rs, rt, y_s.at[0, step - 1], y_r.at[0, step - 1], ydev(1))
        lcp[step] = cop.send(ls, lt, y_s.at[1, step - 1], y_r.at[1, step - 1], ydev(-1))
    rcp[4].wait_recv()
    lcp[4].wait_recv()
    EO[z] = (YP[y].astype(F32) + RR[3].astype(F32) + RL[3].astype(F32)).astype(BF)

    ering = Ring(
        cop, lambda slot, k: EO.at[slot, :, k * 512:(k + 1) * 512], z, zdev(1), zdev(-1), e_s, e_r, 4
    )
    for step in (1, 2, 3, 4):
        ering.forward(step)
    ering.finish()
    for n in range(4):
        cols = slice(n * 512, (n + 1) * 512)
        e = EO[:, :, cols].reshape(NZ * FCAP, 512)
        out[:, cols] = (RES[:, cols] + nn(FG[0], e) + nn(FG[1], e)).astype(BF)

    cop.drain()
    for d in range(1, NX):

        @pl.when(x >= d)
        def _():
            pltpu.make_async_remote_copy(
                src_ref=q, dst_ref=QB.at[d], send_sem=q_s.at[d], recv_sem=q_r.at[d],
                device_id=xdev(-d), device_id_type=MESH,
            ).wait_send()

        @pl.when(x + d < NX)
        def _():
            for src, dst, i in ((OS, OB, 0), (SS, SB, 1)):
                pltpu.make_async_remote_copy(
                    src_ref=src.at[d], dst_ref=dst.at[d], send_sem=o_s.at[d, i], recv_sem=o_r.at[d, i],
                    device_id=xdev(d), device_id_type=MESH,
                ).wait_send()


def shards(
    residual, queries, keys, values, attn_routes, attn_gates, out_weight, norm_gain,
    ffn_routes, ffn_gates, w_gate, w_up, w_down,
):
    q = jnp.transpose(queries[0], (1, 0, 2)).reshape(2 * TOK, HEAD)
    kv = jnp.stack([keys[0], values[0]])
    meta = jnp.concatenate(
        [attn_routes[0].astype(F32), attn_gates[0], ffn_routes[0].astype(F32), ffn_gates[0]], axis=1
    ).T
    w = out_weight[0]
    wo = jnp.concatenate([w[:512], w[512:]], axis=1)
    zero = jnp.zeros((D, 16), BF)
    gate, up = w_gate[0], w_up[0]
    gu = jnp.concatenate([gate[:, :128], gate[:, 128:], zero, up[:, 128:], zero, up[:, :128]], axis=1)
    vm = pl.BlockSpec(memory_space=pltpu.VMEM)
    hbm = pl.BlockSpec(memory_space=pl.ANY)
    dma = lambda *s: pltpu.SemaphoreType.DMA(s)
    vb = lambda *s: pltpu.VMEM(s, BF)
    vf = lambda *s: pltpu.VMEM(s, F32)
    out = pl.pallas_call(
        layer_kernel,
        name="layer",
        out_shape=jax.ShapeDtypeStruct((TOK, D), BF),
        in_specs=[vm, vm, vm, vm, vm, hbm, hbm, hbm],
        out_specs=vm,
        scratch_shapes=[
            vb(NY, 2, TOK, HEAD),
            vb(NX, 2 * TOK, HEAD),
            vb(NX, HEAD, 2 * TOK),
            vf(NX, 8, 2 * TOK),
            vb(NX, HEAD, 2 * TOK),
            vf(NX, 8, 2 * TOK),
            vb(NX, NY, 512, HEAD),
            vb(NX, D, 384),
            vb(NX, 176, D),
            vb(NZ, ACAP, HEAD),
            vb(NZ, ACAP, HEAD),
            vb(NZ, ACAP, D),
            vb(2, TOK, NZ * ACAP),
            vb(2, TOK, NZ * FCAP),
            vb(NY, FCAP, D),
            vb(NY, FCAP, D),
            vb(4, FCAP, D),
            vb(4, FCAP, D),
            vb(NZ, FCAP, D),
            vf(TOK, D),
            dma(3),
            dma(2, 4, 2), dma(2, 4, 2),
            dma(NX), dma(NX),
            dma(NX, 2), dma(NX, 2),
            dma(3), dma(3),
            dma(2, 4, 2), dma(2, 4, 2),
            dma(8), dma(8),
            dma(2, 4), dma(2, 4),
            dma(3, 2), dma(3, 2),
            dma(8), dma(8),
            dma(2, 4, 4), dma(2, 4, 4),
            dma(2, 4, 4), dma(2, 4, 4),
            dma(2, 4), dma(2, 4),
            dma(2, 4, 4), dma(2, 4, 4),
        ],
        compiler_params=pltpu.CompilerParams(
            collective_id=0, has_side_effects=True, vmem_limit_bytes=56 * 1024 * 1024
        ),
    )(meta, residual[0], q, kv, norm_gain.reshape(1, D), wo, gu, w_down[0])
    return out[None]


def solution(mesh):
    in_specs = (
        P("dp", "ctx", None),
        P("dp", "ctx", None, "exp"),
        P("dp", "ctx", "exp"),
        P("dp", "ctx", "exp"),
        P("dp", "ctx", None),
        P("dp", "ctx", None),
        P("exp", None, "ctx"),
        P(),
        P("dp", "ctx", None),
        P("dp", "ctx", None),
        P("exp", None, "ctx"),
        P("exp", None, "ctx"),
        P("exp", "ctx", None),
    )
    out_specs = P("dp", "ctx", None)
    return jax.shard_map(shards, mesh=mesh, in_specs=in_specs, out_specs=out_specs, check_vma=False)
```

```python
import functools
import math

import jax
import jax.numpy as jnp
from jax import lax
from jax.experimental import pallas as pl
from jax.experimental.pallas import tpu as pltpu
from jax.sharding import PartitionSpec as P

MESH = pl.DeviceIdType.MESH
BF = jnp.bfloat16
F32 = jnp.float32
NX, NY, NZ = 4, 8, 8
TOK = 128
D = 2048
HEAD = 128
ACAP = 48
FCAP = 32
NEG = -1e30


def nt(a, b):
    return lax.dot_general(a, b, (((1,), (1,)), ((), ())), preferred_element_type=F32)


def tn(a, b):
    return lax.dot_general(a, b, (((0,), (0,)), ((), ())), preferred_element_type=F32)


def nn(a, b):
    return jnp.dot(a, b, preferred_element_type=F32)


def wrap(v, n):
    return lax.rem(v + 2 * n, n)


class Copy:
    def __init__(self, src, dst, ssem, rsem, dev, sends=None, gets=None):
        self.cp = pltpu.make_async_remote_copy(
            src_ref=src, dst_ref=dst, send_sem=ssem, recv_sem=rsem, device_id=dev, device_id_type=MESH
        )
        self.sends, self.gets = sends, gets
        self.done = False

    def _when(self, cond, act):
        if cond is None:
            act()
        else:
            pl.when(cond)(act)

    def start(self):
        self._when(self.sends, self.cp.start)

    def wait_recv(self):
        self.done = True
        self._when(self.gets, self.cp.wait_recv)

    def wait_send(self):
        self._when(self.sends, self.cp.wait_send)


class Copies:
    def __init__(self):
        self.sent = []

    def send(self, src, dst, ssem, rsem, dev, sends=None, gets=None):
        cp = Copy(src, dst, ssem, rsem, dev, sends, gets)
        cp.start()
        self.sent.append(cp)
        return cp

    def drain(self):
        for cp in self.sent:
            if not cp.done:
                cp.wait_recv()
        for cp in self.sent:
            cp.wait_send()


class Ring:
    def __init__(self, copies, at, pos, right, left, ssem, rsem, chunks):
        self.copies, self.at, self.pos = copies, at, pos
        self.devs = (right, left)
        self.ssem, self.rsem, self.chunks = ssem, rsem, chunks
        self.cps = {}

    def carries(self, way, step, j):
        return step < 4 or (j < self.chunks // 2) == (way == 0)

    def slot(self, way, step):
        return wrap(self.pos - step if way == 0 else self.pos + step, 8)

    def start(self, step, j):
        for way in (0, 1):
            if self.carries(way, step, j):
                slot = self.slot(way, step - 1)
                src = self.at(slot, j)
                self.cps[way, step, j] = self.copies.send(
                    src, self.at(slot, j), self.ssem.at[way, step - 1, j], self.rsem.at[way, step - 1, j], self.devs[way]
                )

    def wait(self, step, j):
        for way in (0, 1):
            if self.carries(way, step, j):
                self.cps[way, step, j].wait_recv()

    def forward(self, step, js=None):
        for j in range(self.chunks) if js is None else js:
            if step > 1:
                self.wait(step - 1, j)
            self.start(step, j)

    def finish(self):
        for j in range(self.chunks):
            self.wait(4, j)


class Two:
    def __init__(self, copies, at, pos, dev, ssem, rsem):
        self.copies, self.at, self.pos, self.dev = copies, at, pos, dev
        self.ssem, self.rsem = ssem, rsem
        self.cps = {}

    def _send(self, way, n, ref, k):
        sign = 1 if way == 0 else -1
        self.cps[way, n] = self.copies.send(
            ref, ref, self.ssem.at[way, n - 1], self.rsem.at[way, n - 1], self.dev(sign * k)
        )

    def start(self):
        for k in (2, 1):
            for way in (0, 1):
                self._send(way, k, self.at(self.pos, None), k)

    def forward(self):
        for way in (0, 1):
            self.cps[way, 2].wait_recv()
        for way in (0, 1):
            slot = wrap(self.pos - 2 if way == 0 else self.pos + 2, 8)
            self._send(way, 4, self.at(slot, way), 2)
            self._send(way, 3, self.at(slot, None), 1)

    def wait(self, *ns):
        for n in ns:
            for way in (0, 1):
                self.cps[way, n].wait_recv()


class Rounds:
    def __init__(self, copies, at, pos, dev, ssem, rsem, chunks):
        self.copies, self.at, self.pos, self.dev = copies, at, pos, dev
        self.ssem, self.rsem, self.chunks = ssem, rsem, chunks
        self.cps = {}

    def _send(self, way, n, j, slot, k):
        ref = self.at(slot, j)
        self.cps[way, n, j] = self.copies.send(
            ref, ref, self.ssem.at[way, n - 1, j], self.rsem.at[way, n - 1, j],
            self.dev(k if way == 0 else -k),
        )

    def start(self, *js):
        for j in js:
            for k in (2, 1):
                for way in (0, 1):
                    self._send(way, k, j, self.pos, k)

    def forward(self, *js):
        for j in js:
            for way in (0, 1):
                self.cps[way, 2, j].wait_recv()
                slot = wrap(self.pos - 2 if way == 0 else self.pos + 2, 8)
                if (j < self.chunks // 2) == (way == 0):
                    self._send(way, 4, j, slot, 2)
                self._send(way, 3, j, slot, 1)

    def wait(self, *js):
        for j in js:
            for n in (1, 3, 4):
                for way in (0, 1):
                    if (way, n, j) in self.cps:
                        self.cps[way, n, j].wait_recv()


def layer_kernel(
    res, q, kk, vv, ar, ag, fr, fg, gain, wo, wg, wu, wd, out,
    RB, QV, AR, AG, FR, FGT, GN, KV, QB, OA, ML, OB, SB, OS, SS, WO, W, PK, ER, PR, PT, MG, FG, XN, XR, YP, RR, RL,
    EO, RES,
    l_s, kv_s, kv_r, q_s, q_r, o_s, o_r, wb_s, wb_r, wz_s, wz_r, wc_s, wc_r,
    fx_s, fx_r, fa_s, fa_r, fc_s, fc_r, a_s, a_r, p_s, p_r, x_s, x_r, y_s, y_r, e_s, e_r,
):
    j = lax.axis_index("dp")
    c = lax.axis_index("ctx")
    z = lax.axis_index("exp")
    x = c // NY
    y = c % NY
    cop = Copies()

    def xdev(k):
        return (j, wrap(x + k, NX) * NY + y, z)

    def ydev(k):
        return (j, x * NY + wrap(y + k, NY), z)

    def zdev(k):
        return (j, c, wrap(z + k, NZ))

    sib = (1 - j, c, z)

    def part(n, i):
        return pl.ds(pl.multiple_of(i * n, n), n)

    barrier = pltpu.get_barrier_semaphore()
    partners = [xdev(k) for k in (1, 2, 3)] + [ydev(k) for k in (1, 2, -2, -1)] + [zdev(k) for k in range(1, 8)] + [sib]
    for dev in partners:
        pl.semaphore_signal(barrier, inc=1, device_id=dev, device_id_type=MESH)

    local = [
        (kk, KV.at[y, 0]), (vv, KV.at[y, 1]), (q, QV),
        (ar, AR), (ag, AG), (fr, FR), (fg, FGT),
        (res, RB), (gain, GN),
        (wo.at[:, part(512, j)], WO.at[x, y, :, part(512, j)]),
        (wg, W.at[0, x]), (wu, W.at[1, x]), (wd, W.at[2, x]),
    ]
    own_w = [pltpu.make_async_copy(src, dst, l_s.at[i]) for i, (src, dst) in enumerate(local)]

    def wait_local(*ids):
        for i in ids:
            own_w[i].wait()

    for cp in own_w:
        cp.start()
    pl.semaphore_wait(barrier, len(partners))

    lanes = part(512, j)
    wait_local(0, 1)
    kvring = Two(
        cop, lambda slot, h: KV.at[slot] if h is None else KV.at[slot, h], y, ydev, kv_s, kv_r
    )
    kvring.start()
    qcp = {
        d: cop.send(q, QB.at[d], q_s.at[d], q_r.at[d], xdev(-d), sends=x >= d, gets=x + d < NX)
        for d in (3, 2, 1)
    }

    def block(slot, h):
        if h is None:
            return WO.at[x, slot, :, lanes]
        return WO.at[x, slot, 32 * h:32 * h + 32, lanes]

    wb = Two(cop, block, y, ydev, wb_s, wb_r)
    wz = {}
    wcs = []

    def to_sibling(*slots):
        for slot in slots:
            n = len(wcs)
            ref = WO.at[slot, :, :, lanes]
            wcs.append(cop.send(ref, ref, wc_s.at[n], wc_r.at[n], sib))

    def along_x(*ns):
        for n in ns:
            slot = wrap(y + n, NY)
            for way, step in ((0, 1), (1, -1)):
                wz[way, 0, n] = cop.send(
                    wo.at[:, lanes] if n == 0 else WO.at[x, slot, :, lanes], WO.at[x, slot, :, lanes],
                    wz_s.at[way, 0, n], wz_r.at[way, 0, n], xdev(step),
                )

    def along_x_again(*ns):
        for n in ns:
            slot = wrap(y + n, NY)
            for way, step in ((0, 1), (1, -1)):
                wz[way, 0, n].wait_recv()
                ref = WO.at[wrap(x - step, NX), slot, 32 * way:32 * way + 32, lanes]
                wz[way, 1, n] = cop.send(ref, ref, wz_s.at[way, 1, n], wz_r.at[way, 1, n], xdev(step))

    along_x(0)

    quarter = [pl.ds(pl.multiple_of(j * 1024 + h * 512, 512), 512) for h in (0, 1)]
    fx = {}

    def send_weights(which):
        for turn in (0, 1):
            for way, step in ((0, 1), (1, -1)):
                h = turn if way == 0 else 1 - turn
                for i in which:
                    fx[way, i, h] = cop.send(
                        (wg, wu, wd)[i].at[:, quarter[h]], W.at[i, x, :, quarter[h]],
                        fx_s.at[way, i, h], fx_r.at[way, i, h], xdev(step),
                    )

    fa = {}

    def forward_weights(which):
        for way, step in ((0, 1), (1, -1)):
            slot = wrap(x - step, NX)
            for i in which:
                fx[way, i, way].wait_recv()
                ref = W.at[i, slot, :, quarter[way]]
                fa[way, i] = cop.send(ref, ref, fa_s.at[way, i], fa_r.at[way, i], xdev(step))

    fcs = []

    def weights_to_sibling(n, which, slot):
        for i in which:
            ref = W.at[i, slot, :, part(1024, j)]
            fcs.append(cop.send(ref, ref, fc_s.at[n, i], fc_r.at[n, i], sib))

    def near_to_sibling(which):
        for way, step in ((0, 1), (1, -1)):
            for i in which:
                fx[way, i, 1 - way].wait_recv()
            weights_to_sibling(way, which, wrap(x - step, NX))

    def far_to_sibling(which):
        for i in which:
            for way in (0, 1):
                fa[way, i].wait_recv()
        weights_to_sibling(2, which, wrap(x + 2, NX))

    send_weights((0,))

    factor = math.log2(math.e) / math.sqrt(HEAD)

    def absorb(d, blocks, first=False, last=False):
        queries = QV[...] if d == 0 else QB[d]
        ks = jnp.concatenate([KV[b, 0] for b in blocks], axis=0)
        vs = jnp.concatenate([KV[b, 1] for b in blocks], axis=0)
        s = nt(ks, queries) * factor
        if d == 0:
            row = lax.broadcasted_iota(jnp.int32, (TOK, 2 * TOK), 0)
            qpos = y * TOK + lax.shift_right_logical(
                lax.broadcasted_iota(jnp.int32, (TOK, 2 * TOK), 1), 1
            )
            allowed = jnp.concatenate([row + b * TOK - qpos for b in blocks], axis=0) <= 0
            s = jnp.where(allowed, s, NEG)
        m = jnp.max(s, axis=0, keepdims=True)
        if not first:
            old = ML[d, 0:1, :]
            m = jnp.maximum(m, old)
        p = jnp.exp2(s - m)
        l = jnp.sum(p, axis=0, keepdims=True)
        o = tn(vs, p.astype(BF))
        if not first:
            shrink = jnp.exp2(old - m)
            l = l + ML[d, 1:2, :] * shrink
            o = o + OA[d] * shrink
        if last:
            return o, m, l
        ML[d, 0:1, :] = m
        ML[d, 1:2, :] = l
        OA[d] = o

    def absorb_later(blocks, first=False):
        for d in range(1, NX):

            @pl.when(x + d < NX)
            def _():
                absorb(d, blocks, first)

    def pair(step):
        return [wrap(y - step, NY), wrap(y + step, NY)]

    wait_local(2, 9)
    absorb(0, [y], first=True)
    wb.start()

    wait_local(3, 4, 5, 6)
    upper = (
        lax.broadcasted_iota(jnp.int32, (256, 256), 0) < lax.broadcasted_iota(jnp.int32, (256, 256), 1)
    ).astype(F32).astype(BF)

    def ranks(route):
        eid = lax.broadcasted_iota(jnp.int32, (8, 256), 0).astype(F32)
        onehot = (eid == route).astype(F32)
        before = nn(onehot.astype(BF), upper)
        return jnp.sum(before * onehot, axis=0, keepdims=True)

    def iota0(rows, cols):
        return lax.broadcasted_iota(jnp.int32, (rows, cols), 0).astype(F32)

    def gate_table(slot, gates, rows):
        rid = iota0(rows, TOK)
        t = jnp.where(rid == slot[:, :TOK], gates[0:1, :], 0.0) + jnp.where(
            rid == slot[:, TOK:], gates[1:2, :], 0.0
        )
        t = t.T
        hi = t.astype(BF)
        return hi, (t - hi.astype(F32)).astype(BF)

    aroute = AR[...].astype(F32)
    aroute = jnp.concatenate([aroute[0:1, :], aroute[1:2, :]], axis=1)
    arank = ranks(aroute)
    by_slot = (iota0(8 * ACAP, 256) == aroute * ACAP + arank).astype(F32).astype(BF)
    src = lax.broadcasted_iota(jnp.int32, (256, 256), 0)
    dst = 2 * jnp.bitwise_and(src, TOK - 1) + lax.shift_right_logical(src, 7)
    swap = (lax.broadcasted_iota(jnp.int32, (256, 256), 1) == dst).astype(F32).astype(BF)
    disp = nn(by_slot, swap).astype(BF)
    main = aroute * 32 + arank
    extra = 256 + aroute * 16 + (arank - 32)
    agates = AG[...]
    for i in range(2):
        MG[2 * i], MG[2 * i + 1] = gate_table(jnp.where(arank < 32, main, extra + 8 * i), agates, 384)

    froute = FR[...].astype(F32)
    froute = jnp.concatenate([froute[0:1, :], froute[1:2, :]], axis=1)
    fslot = froute * FCAP + ranks(froute)
    FG[0], FG[1] = gate_table(fslot, FGT[...], 8 * FCAP)
    mine = iota0(FCAP, TOK) + (z * FCAP).astype(F32)
    sel = ((mine == fslot[:, :TOK]).astype(F32) + (mine == fslot[:, TOK:]).astype(F32)).astype(BF)

    kvring.forward()
    kvring.wait(1)
    near = pair(1) + pair(2)
    absorb(0, near)
    for d in range(1, NX):
        qcp[d].wait_recv()
    absorb_later([y] + near, first=True)
    wb.forward()
    wb.wait(1)
    along_x(1, 7, 2, 6)
    kvring.wait(3, 4)
    ocp = []
    final = pair(3) + [wrap(y + 4, NY)]
    for d in (3, 2, 1):

        @pl.when(x + d < NX)
        def _():
            o, m, l = absorb(d, final, last=True)
            OS[d] = o.astype(BF)
            SS[d] = jnp.concatenate([m, l, jnp.zeros((6, 2 * TOK), F32)], axis=0)

        for src, dst, i in ((OS, OB, 0), (SS, SB, 1)):
            ocp.append(
                cop.send(
                    src.at[d], dst.at[d], o_s.at[d, i], o_r.at[d, i], xdev(d),
                    sends=x + d < NX, gets=x >= d,
                )
            )
    o, m, l = absorb(0, final, last=True)
    wb.wait(3, 4)
    along_x(3, 5, 4)
    to_sibling(x)
    along_x_again(0, 1, 7, 2, 6)
    for cp in ocp:
        cp.wait_recv()
    tops = [jnp.where(x >= d, SB[d, 0:1, :], NEG) for d in range(1, NX)]
    top = m
    for t in tops:
        top = jnp.maximum(top, t)
    f = jnp.exp2(m - top)
    o = o * f
    l = l * f
    for d in range(1, NX):
        f = jnp.exp2(tops[d - 1] - top)
        o = o + jnp.where(x >= d, OB[d].astype(F32), 0.0) * f
        l = l + jnp.where(x >= d, SB[d, 1:2, :], 0.0) * f
    attended = (o / l).astype(BF)

    PK[...] = nt(disp, attended).astype(BF).reshape(NZ, ACAP, HEAD)
    acps = [cop.send(PK.at[wrap(z + k, NZ)], ER.at[z], a_s.at[k], a_r.at[k], zdev(k)) for k in range(1, NZ)]
    ER[z] = PK[z]
    along_x_again(3, 5, 4)
    to_sibling(wrap(x - 1, NX), wrap(x + 1, NX))
    forward_weights((0,))
    send_weights((1, 2))
    for cp in acps:
        cp.wait_recv()
    lhs = jnp.concatenate([ER[h] for h in range(NZ)], axis=1)
    order = [x, wrap(x - 1, NX), wrap(x + 1, NX), wrap(x + 2, NX)]
    real = [part(512, b) for b in order]
    ends = {}

    def project(n):
        wcs[n].wait_recv()
        r = nt(lhs, WO[order[n]].reshape(512, 1024))
        PR[z, :, n * 512:(n + 1) * 512] = r[0:32].astype(BF)
        ends[n] = r[32:40]
        if n % 2 == 1:
            k = n // 2
            PT[z, :, k * 512:(k + 1) * 512] = jnp.concatenate([ends[n - 1], ends[n]], axis=0).astype(BF)
            pring.start(2 * k, 2 * k + 1)

    def wide(slot, k):
        h = (k // 2) * 1024
        return PR.at[slot, :, h:h + 1024] if k % 2 == 0 else PT.at[slot, :, h // 2:h // 2 + 512]

    pring = Rounds(cop, wide, z, zdev, p_s, p_r, 4)
    A, B = (0, 1), (2, 3)
    project(0)
    project(1)
    project(2)
    wait_local(7, 8)
    tables = [nn(sel, MG[i]).astype(BF) for i in range(4)]
    picked = [nn(sel, RB[:, real[n]]) for n in range(4)]
    pring.forward(*A)
    for way in (0, 1):
        for n in range(NY):
            wz[way, 1, n].wait_recv()
    to_sibling(wrap(x + 2, NX))
    project(3)
    pring.forward(*B)

    def projected(n):
        t = (n // 2) * 512
        return jnp.concatenate(
            [
                PR[:, :, n * 512:(n + 1) * 512].reshape(256, 512),
                PT[:, :, t:t + 512].reshape(128, 512),
            ],
            axis=0,
        )

    xring = Rounds(
        cop, lambda slot, k: XN.at[slot, :, k * 512:(k + 1) * 512], y, ydev, x_s, x_r, 4
    )

    def pick(group):
        pring.wait(*group)
        for n in group:
            rows = projected(n)
            h = 2 * (n % 2)
            XN[y, :, n * 512:(n + 1) * 512] = (
                picked[n] + nn(tables[h], rows) + nn(tables[h + 1], rows)
            ).astype(BF)
            xring.start(n)

    pick(A)
    pick(B)
    xring.forward(*A)

    def normalise(slot):
        v = XN[slot].astype(F32)
        scale = lax.rsqrt(jnp.mean(v * v, axis=1, keepdims=True) + 1e-6)
        for n in range(4):
            XR[slot, :, real[n]] = (v[:, n * 512:(n + 1) * 512] * scale * GN[:, real[n]]).astype(BF)

    near_to_sibling((0,))
    forward_weights((1, 2))
    near_to_sibling((1, 2))
    normalise(y)
    xring.forward(*B)
    for n in range(4):
        rows = projected(n)
        h = 2 * (n % 2)
        RES[:, real[n]] = RB[:, real[n]].astype(F32) + nn(MG[h], rows) + nn(MG[h + 1], rows)
    far_to_sibling((0,))
    xring.wait(*A, *B)
    for slot in pair(1) + pair(2) + pair(3) + [wrap(y + 4, NY)]:
        normalise(slot)
    wait_local(10, 11, 12)
    for cp in fcs:
        cp.wait_recv()
    fcs.clear()
    far_to_sibling((1, 2))
    for cp in fcs:
        cp.wait_recv()
    fcs.clear()
    rows = XR[...].reshape(NY * FCAP, D)
    hidden = []
    for n in (0, 256, 512):
        size = min(256, 704 - n)
        g = nt(rows, W[0].reshape(704, D)[n:n + size])
        u = nt(rows, W[1].reshape(704, D)[n:n + size])
        hidden.append((g / (1.0 + jnp.exp(-g)) * u).astype(BF))
    hidden = jnp.concatenate(hidden, axis=1)

    def cut(ref, k, n):
        return ref.at[k, :, n * 512:(n + 1) * 512]

    hop = {}

    def pass_on(way, near, n, dest, k):
        sign = 1 if way == 0 else -1
        hop[way, near, n] = cop.send(
            cut(YP, wrap(y + sign * dest, NY), n), cut((RR, RL)[way], near, n),
            y_s.at[way, near, n], y_r.at[way, near, n], ydev(sign * k),
        )

    for n in range(4):
        cols = slice(n * 512, (n + 1) * 512)
        YP[:, :, cols] = nn(hidden, W[2, :, :, cols].reshape(704, 512)).astype(BF).reshape(NY, FCAP, 512)
        pass_on(n // 2, 3, n, 4, 2)
        for way in (0, 1):
            pass_on(way, 2, n, 3, 1)
    for n in range(4):
        cols = slice(n * 512, (n + 1) * 512)
        for way in (0, 1):
            got = (RR, RL)[way]
            dest = wrap(y + 2 if way == 0 else y - 2, NY)
            hop[way, 2, n].wait_recv()
            share = YP[dest, :, cols].astype(F32) + got[2, :, cols].astype(F32)
            if way == n // 2:
                hop[way, 3, n].wait_recv()
                share = share + got[3, :, cols].astype(F32)
            YP[dest, :, cols] = share.astype(BF)
            pass_on(way, 1, n, 2, 2)
        for way in (0, 1):
            pass_on(way, 0, n, 1, 1)
    ering = Rounds(
        cop, lambda slot, k: EO.at[slot, :, k * 512:(k + 1) * 512], z, zdev, e_s, e_r, 4
    )
    for n in range(4):
        cols = slice(n * 512, (n + 1) * 512)
        total = YP[y, :, cols].astype(F32)
        for way in (0, 1):
            for near in (0, 1):
                hop[way, near, n].wait_recv()
                total = total + (RR, RL)[way][near, :, cols].astype(F32)
        EO[z, :, cols] = total.astype(BF)
        ering.start(n)
    ering.forward(*A, *B)
    for n in range(4):
        cols = slice(n * 512, (n + 1) * 512)
        ering.wait(n)
        e = EO[:, :, cols].reshape(NZ * FCAP, 512)
        out[:, cols] = (RES[:, cols] + nn(FG[0], e) + nn(FG[1], e)).astype(BF)

    cop.drain()


def shards(
    residual, queries, keys, values, attn_routes, attn_gates, out_weight, norm_gain,
    ffn_routes, ffn_gates, w_gate, w_up, w_down,
):
    hbm = pl.BlockSpec(memory_space=pl.ANY)
    dma = lambda *s: pltpu.SemaphoreType.DMA(s)
    vb = lambda *s: pltpu.VMEM(s, BF)
    vf = lambda *s: pltpu.VMEM(s, F32)
    vi = lambda *s: pltpu.VMEM(s, jnp.int32)
    out = pl.pallas_call(
        layer_kernel,
        name="layer",
        out_shape=jax.ShapeDtypeStruct((TOK, D), BF),
        in_specs=[hbm] * 13,
        out_specs=pl.BlockSpec(memory_space=pltpu.VMEM),
        scratch_shapes=[
            vb(TOK, D),
            vb(2 * TOK, HEAD),
            vi(2, TOK), vf(2, TOK), vi(2, TOK), vf(2, TOK),
            vf(1, D),
            vb(NY, 2, TOK, HEAD),
            vb(NX, 2 * TOK, HEAD),
            vf(NX, HEAD, 2 * TOK),
            vf(NX, 8, 2 * TOK),
            vb(NX, HEAD, 2 * TOK),
            vf(NX, 8, 2 * TOK),
            vb(NX, HEAD, 2 * TOK),
            vf(NX, 8, 2 * TOK),
            vb(NX, NY, 64, 1024),
            vb(3, NX, 176, D),
            vb(NZ, ACAP, HEAD),
            vb(NZ, ACAP, HEAD),
            vb(NZ, 32, D),
            vb(NZ, 16, 1024),
            vb(4, TOK, 384),
            vb(2, TOK, NZ * FCAP),
            vb(NY, FCAP, D),
            vb(NY, FCAP, D),
            vb(NY, FCAP, D),
            vb(4, FCAP, D),
            vb(4, FCAP, D),
            vb(NZ, FCAP, D),
            vf(TOK, D),
            dma(13),
            dma(2, 4), dma(2, 4),
            dma(NX), dma(NX),
            dma(NX, 2), dma(NX, 2),
            dma(2, 4), dma(2, 4),
            dma(2, 2, 8), dma(2, 2, 8),
            dma(4), dma(4),
            dma(2, 3, 2), dma(2, 3, 2),
            dma(2, 3), dma(2, 3),
            dma(3, 3), dma(3, 3),
            dma(8), dma(8),
            dma(2, 4, 4), dma(2, 4, 4),
            dma(2, 4, 4), dma(2, 4, 4),
            dma(2, 4, 4), dma(2, 4, 4),
            dma(2, 4, 4), dma(2, 4, 4),
        ],
        compiler_params=pltpu.CompilerParams(
            collective_id=0, has_side_effects=True, vmem_limit_bytes=56 * 1024 * 1024
        ),
    )(
        residual[0], queries[0].reshape(2 * TOK, HEAD), keys[0], values[0],
        attn_routes[0].T, attn_gates[0].T, ffn_routes[0].T, ffn_gates[0].T,
        norm_gain.reshape(1, D), out_weight[0].T, w_gate[0].T, w_up[0].T, w_down[0],
    )
    return out[None]


def solution(mesh):
    in_specs = (
        P("dp", "ctx", None),
        P("dp", "ctx", None, "exp"),
        P("dp", "ctx", "exp"),
        P("dp", "ctx", "exp"),
        P("dp", "ctx", None),
        P("dp", "ctx", None),
        P("exp", None, "ctx"),
        P(),
        P("dp", "ctx", None),
        P("dp", "ctx", None),
        P("exp", None, "ctx"),
        P("exp", None, "ctx"),
        P("exp", "ctx", None),
    )
    out_specs = P("dp", "ctx", None)
    return jax.shard_map(shards, mesh=mesh, in_specs=in_specs, out_specs=out_specs, check_vma=False)
```

```python
import functools
import math

import jax
import jax.numpy as jnp
from jax import lax
from jax.experimental import pallas as pl
from jax.experimental.pallas import tpu as pltpu
from jax.sharding import PartitionSpec as P

MESH = pl.DeviceIdType.MESH
BF = jnp.bfloat16
F32 = jnp.float32
NX, NY, NZ = 4, 8, 8
TOK = 128
D = 2048
HEAD = 128
ACAP = 48
FCAP = 32
NEG = -1e30


def nt(a, b):
    return lax.dot_general(a, b, (((1,), (1,)), ((), ())), preferred_element_type=F32)


def tn(a, b):
    return lax.dot_general(a, b, (((0,), (0,)), ((), ())), preferred_element_type=F32)


def nn(a, b):
    return jnp.dot(a, b, preferred_element_type=F32)


def wrap(v, n):
    return lax.rem(v + 2 * n, n)


class Copy:
    def __init__(self, src, dst, ssem, rsem, dev, sends=None, gets=None):
        self.cp = pltpu.make_async_remote_copy(
            src_ref=src, dst_ref=dst, send_sem=ssem, recv_sem=rsem, device_id=dev, device_id_type=MESH
        )
        self.sends, self.gets = sends, gets
        self.done = self.left = False

    def _when(self, cond, act):
        if cond is None:
            act()
        else:
            pl.when(cond)(act)

    def start(self):
        self._when(self.sends, self.cp.start)

    def wait_recv(self):
        self.done = True
        self._when(self.gets, self.cp.wait_recv)

    def wait_send(self):
        if not self.left:
            self.left = True
            self._when(self.sends, self.cp.wait_send)


class Copies:
    def __init__(self):
        self.sent = []

    def send(self, src, dst, ssem, rsem, dev, sends=None, gets=None):
        cp = Copy(src, dst, ssem, rsem, dev, sends, gets)
        cp.start()
        self.sent.append(cp)
        return cp

    def drain(self):
        for cp in self.sent:
            if not cp.done:
                cp.wait_recv()
        self.flush()

    def flush(self):
        for cp in self.sent:
            cp.wait_send()
        self.sent = [cp for cp in self.sent if not cp.done]


class Ring:
    def __init__(self, copies, at, pos, right, left, ssem, rsem, chunks):
        self.copies, self.at, self.pos = copies, at, pos
        self.devs = (right, left)
        self.ssem, self.rsem, self.chunks = ssem, rsem, chunks
        self.cps = {}

    def carries(self, way, step, j):
        return step < 4 or (j < self.chunks // 2) == (way == 0)

    def slot(self, way, step):
        return wrap(self.pos - step if way == 0 else self.pos + step, 8)

    def start(self, step, j):
        for way in (0, 1):
            if self.carries(way, step, j):
                slot = self.slot(way, step - 1)
                src = self.at(slot, j)
                self.cps[way, step, j] = self.copies.send(
                    src, self.at(slot, j), self.ssem.at[way, step - 1, j], self.rsem.at[way, step - 1, j], self.devs[way]
                )

    def wait(self, step, j):
        for way in (0, 1):
            if self.carries(way, step, j):
                self.cps[way, step, j].wait_recv()

    def forward(self, step, js=None):
        for j in range(self.chunks) if js is None else js:
            if step > 1:
                self.wait(step - 1, j)
            self.start(step, j)

    def finish(self):
        for j in range(self.chunks):
            self.wait(4, j)


class Two:
    def __init__(self, copies, at, pos, dev, ssem, rsem):
        self.copies, self.at, self.pos, self.dev = copies, at, pos, dev
        self.ssem, self.rsem = ssem, rsem
        self.cps = {}

    def _send(self, way, n, ref, k):
        sign = 1 if way == 0 else -1
        self.cps[way, n] = self.copies.send(
            ref, ref, self.ssem.at[way, n - 1], self.rsem.at[way, n - 1], self.dev(sign * k)
        )

    def start(self):
        for k in (2, 1):
            for way in (0, 1):
                self._send(way, k, self.at(self.pos, None), k)

    def forward(self):
        for way in (0, 1):
            self.cps[way, 2].wait_recv()
        for way in (0, 1):
            slot = wrap(self.pos - 2 if way == 0 else self.pos + 2, 8)
            self._send(way, 4, self.at(slot, way), 2)
            self._send(way, 3, self.at(slot, None), 1)

    def wait(self, *ns):
        for n in ns:
            for way in (0, 1):
                self.cps[way, n].wait_recv()


class Rounds:
    def __init__(self, copies, at, pos, dev, ssem, rsem, chunks):
        self.copies, self.at, self.pos, self.dev = copies, at, pos, dev
        self.ssem, self.rsem, self.chunks = ssem, rsem, chunks
        self.cps = {}

    def _send(self, way, n, j, slot, k):
        ref = self.at(slot, j)
        self.cps[way, n, j] = self.copies.send(
            ref, ref, self.ssem.at[way, n - 1, j], self.rsem.at[way, n - 1, j],
            self.dev(k if way == 0 else -k),
        )

    def start(self, *js):
        for j in js:
            for k in (2, 1):
                for way in (0, 1):
                    self._send(way, k, j, self.pos, k)

    def forward(self, *js):
        for j in js:
            for way in (0, 1):
                self.cps[way, 2, j].wait_recv()
                slot = wrap(self.pos - 2 if way == 0 else self.pos + 2, 8)
                if (j < self.chunks // 2) == (way == 0):
                    self._send(way, 4, j, slot, 2)
                self._send(way, 3, j, slot, 1)

    def wait(self, *js):
        for j in js:
            for n in (1, 3, 4):
                for way in (0, 1):
                    if (way, n, j) in self.cps:
                        self.cps[way, n, j].wait_recv()


def layer_kernel(
    res, q, kk, vv, ar, ag, fr, fg, gain, wo, wg, wu, wd, out,
    RB, QV, AR, AG, FR, FGT, GN, KV, QB, OA, ML, OB, SB, OS, SS, WO, W, PK, ER, PR, PT, MG, FG, XN, XR, YP, RR, RL,
    EO, RES,
    l_s, kv_s, kv_r, q_s, q_r, o_s, o_r, wb_s, wb_r, wy_s, wy_r, wz_s, wz_r, wc_s, wc_r,
    fx_s, fx_r, fa_s, fa_r, fc_s, fc_r, a_s, a_r, p_s, p_r, x_s, x_r, y_s, y_r, e_s, e_r,
):
    j = lax.axis_index("dp")
    c = lax.axis_index("ctx")
    z = lax.axis_index("exp")
    x = c // NY
    y = c % NY
    cop = Copies()

    def xdev(k):
        return (j, wrap(x + k, NX) * NY + y, z)

    def ydev(k):
        return (j, x * NY + wrap(y + k, NY), z)

    def zdev(k):
        return (j, c, wrap(z + k, NZ))

    sib = (1 - j, c, z)

    def part(n, i):
        return pl.ds(pl.multiple_of(i * n, n), n)

    barrier = pltpu.get_barrier_semaphore()
    partners = [xdev(k) for k in (1, 2, 3)] + [ydev(k) for k in (1, 2, -2, -1)] + [zdev(k) for k in range(1, 8)] + [sib]
    for dev in partners:
        pl.semaphore_signal(barrier, inc=1, device_id=dev, device_id_type=MESH)

    local = [
        (kk, KV.at[y, 0]), (vv, KV.at[y, 1]), (q, QV),
        (ar, AR), (ag, AG), (fr, FR), (fg, FGT),
        (res, RB), (gain, GN),
        (wo.at[:, part(512, j)], WO.at[x, y, :, part(512, j)]),
        (wg, W.at[0, x]), (wu, W.at[1, x]), (wd, W.at[2, x]),
    ]
    own_w = [pltpu.make_async_copy(src, dst, l_s.at[i]) for i, (src, dst) in enumerate(local)]

    def wait_local(*ids):
        for i in ids:
            own_w[i].wait()

    for cp in own_w:
        cp.start()
    pl.semaphore_wait(barrier, len(partners))

    lanes = part(512, j)
    wait_local(0, 1)
    kvring = Two(
        cop, lambda slot, h: KV.at[slot] if h is None else KV.at[slot, h], y, ydev, kv_s, kv_r
    )
    kvring.start()
    qcp = {
        d: cop.send(q, QB.at[d], q_s.at[d], q_r.at[d], xdev(-d), sends=x >= d, gets=x + d < NX)
        for d in (3, 2, 1)
    }

    def block(slot, h):
        if h is None:
            return WO.at[x, slot, :, lanes]
        return WO.at[x, slot, 32 * h:32 * h + 32, lanes]

    far = wrap(x + 2, NX)

    def far_block(slot, h):
        if h is None:
            return WO.at[far, slot, :, lanes]
        return WO.at[far, slot, 32 * h:32 * h + 32, lanes]

    wb = Two(cop, block, y, ydev, wb_s, wb_r)
    wf = Two(cop, far_block, y, ydev, wy_s, wy_r)
    wz = {}
    wcs = []

    def to_sibling(*slots):
        for slot in slots:
            n = len(wcs)
            ref = WO.at[slot, :, :, lanes]
            wcs.append(cop.send(ref, ref, wc_s.at[n], wc_r.at[n], sib))

    def along_x(*ns):
        for n in ns:
            slot = wrap(y + n, NY)
            for way, step in ((0, 1), (1, -1)):
                wz[way, 0, n] = cop.send(
                    wo.at[:, lanes] if n == 0 else WO.at[x, slot, :, lanes], WO.at[x, slot, :, lanes],
                    wz_s.at[way, 0, n], wz_r.at[way, 0, n], xdev(step),
                )

    along_x(0)
    across = cop.send(wo.at[:, lanes], WO.at[x, y, :, lanes], wz_s.at[0, 1, 0], wz_r.at[0, 1, 0], xdev(2))

    quarter = [pl.ds(pl.multiple_of(j * 1024 + h * 512, 512), 512) for h in (0, 1)]
    fx = {}

    def send_weights(which):
        for turn in (0, 1):
            for way, step in ((0, 1), (1, -1)):
                h = turn if way == 0 else 1 - turn
                for i in which:
                    fx[way, i, h] = cop.send(
                        (wg, wu, wd)[i].at[:, quarter[h]], W.at[i, x, :, quarter[h]],
                        fx_s.at[way, i, h], fx_r.at[way, i, h], xdev(step),
                    )

    fa = {}

    def forward_weights(which):
        for way, step in ((0, 1), (1, -1)):
            slot = wrap(x - step, NX)
            for i in which:
                fx[way, i, way].wait_recv()
                ref = W.at[i, slot, :, quarter[way]]
                fa[way, i] = cop.send(ref, ref, fa_s.at[way, i], fa_r.at[way, i], xdev(step))

    fcs = []

    def weights_to_sibling(n, which, slot):
        for i in which:
            ref = W.at[i, slot, :, part(1024, j)]
            fcs.append(cop.send(ref, ref, fc_s.at[n, i], fc_r.at[n, i], sib))

    def near_to_sibling(which):
        for way, step in ((0, 1), (1, -1)):
            for i in which:
                fx[way, i, 1 - way].wait_recv()
            weights_to_sibling(way, which, wrap(x - step, NX))

    def far_to_sibling(which):
        for i in which:
            for way in (0, 1):
                fa[way, i].wait_recv()
        weights_to_sibling(2, which, wrap(x + 2, NX))

    send_weights((0,))

    factor = math.log2(math.e) / math.sqrt(HEAD)

    def absorb(d, blocks, first=False, last=False):
        queries = QV[...] if d == 0 else QB[d]
        ks = jnp.concatenate([KV[b, 0] for b in blocks], axis=0)
        vs = jnp.concatenate([KV[b, 1] for b in blocks], axis=0)
        s = nt(ks, queries) * factor
        if d == 0:
            row = lax.broadcasted_iota(jnp.int32, (TOK, 2 * TOK), 0)
            qpos = y * TOK + lax.shift_right_logical(
                lax.broadcasted_iota(jnp.int32, (TOK, 2 * TOK), 1), 1
            )
            allowed = jnp.concatenate([row + b * TOK - qpos for b in blocks], axis=0) <= 0
            s = jnp.where(allowed, s, NEG)
        m = jnp.max(s, axis=0, keepdims=True)
        if not first:
            old = ML[d, 0:1, :]
            m = jnp.maximum(m, old)
        p = jnp.exp2(s - m)
        l = jnp.sum(p, axis=0, keepdims=True)
        o = tn(vs, p.astype(BF))
        if not first:
            shrink = jnp.exp2(old - m)
            l = l + ML[d, 1:2, :] * shrink
            o = o + OA[d] * shrink
        if last:
            return o, m, l
        ML[d, 0:1, :] = m
        ML[d, 1:2, :] = l
        OA[d] = o

    def absorb_later(blocks, first=False):
        for d in range(1, NX):

            @pl.when(x + d < NX)
            def _():
                absorb(d, blocks, first)

    def pair(step):
        return [wrap(y - step, NY), wrap(y + step, NY)]

    wait_local(2, 9)
    absorb(0, [y], first=True)
    wb.start()

    wait_local(3, 4, 5, 6)
    upper = (
        lax.broadcasted_iota(jnp.int32, (256, 256), 0) < lax.broadcasted_iota(jnp.int32, (256, 256), 1)
    ).astype(F32).astype(BF)

    def ranks(route):
        eid = lax.broadcasted_iota(jnp.int32, (8, 256), 0).astype(F32)
        onehot = (eid == route).astype(F32)
        before = nn(onehot.astype(BF), upper)
        return jnp.sum(before * onehot, axis=0, keepdims=True)

    def iota0(rows, cols):
        return lax.broadcasted_iota(jnp.int32, (rows, cols), 0).astype(F32)

    def gate_table(slot, gates, rows):
        rid = iota0(rows, TOK)
        t = jnp.where(rid == slot[:, :TOK], gates[0:1, :], 0.0) + jnp.where(
            rid == slot[:, TOK:], gates[1:2, :], 0.0
        )
        t = t.T
        hi = t.astype(BF)
        return hi, (t - hi.astype(F32)).astype(BF)

    aroute = AR[...].astype(F32)
    aroute = jnp.concatenate([aroute[0:1, :], aroute[1:2, :]], axis=1)
    arank = ranks(aroute)
    by_slot = (iota0(8 * ACAP, 256) == aroute * ACAP + arank).astype(F32).astype(BF)
    src = lax.broadcasted_iota(jnp.int32, (256, 256), 0)
    dst = 2 * jnp.bitwise_and(src, TOK - 1) + lax.shift_right_logical(src, 7)
    swap = (lax.broadcasted_iota(jnp.int32, (256, 256), 1) == dst).astype(F32).astype(BF)
    disp = nn(by_slot, swap).astype(BF)
    main = aroute * 32 + arank
    extra = 256 + aroute * 16 + (arank - 32)
    agates = AG[...]
    for i in range(2):
        MG[2 * i], MG[2 * i + 1] = gate_table(jnp.where(arank < 32, main, extra + 8 * i), agates, 384)

    froute = FR[...].astype(F32)
    froute = jnp.concatenate([froute[0:1, :], froute[1:2, :]], axis=1)
    fslot = froute * FCAP + ranks(froute)
    FG[0], FG[1] = gate_table(fslot, FGT[...], 8 * FCAP)
    mine = iota0(FCAP, TOK) + (z * FCAP).astype(F32)
    sel = ((mine == fslot[:, :TOK]).astype(F32) + (mine == fslot[:, TOK:]).astype(F32)).astype(BF)

    kvring.forward()
    kvring.wait(1)
    near = pair(1) + pair(2)
    absorb(0, near)
    for d in range(1, NX):
        qcp[d].wait_recv()
    absorb_later([y] + near, first=True)
    wb.forward()
    wb.wait(1)
    along_x(1, 7, 2, 6)
    kvring.wait(3, 4)
    across.wait_recv()
    wf.start()
    ocp = []
    final = pair(3) + [wrap(y + 4, NY)]
    for d in (3, 2, 1):

        @pl.when(x + d < NX)
        def _():
            o, m, l = absorb(d, final, last=True)
            OS[d] = o.astype(BF)
            SS[d] = jnp.concatenate([m, l, jnp.zeros((6, 2 * TOK), F32)], axis=0)

        for src, dst, i in ((OS, OB, 0), (SS, SB, 1)):
            ocp.append(
                cop.send(
                    src.at[d], dst.at[d], o_s.at[d, i], o_r.at[d, i], xdev(d),
                    sends=x + d < NX, gets=x >= d,
                )
            )
    o, m, l = absorb(0, final, last=True)
    wb.wait(3, 4)
    along_x(3, 5, 4)
    to_sibling(x)
    wf.forward()
    for cp in ocp:
        cp.wait_recv()
    tops = [jnp.where(x >= d, SB[d, 0:1, :], NEG) for d in range(1, NX)]
    top = m
    for t in tops:
        top = jnp.maximum(top, t)
    f = jnp.exp2(m - top)
    o = o * f
    l = l * f
    for d in range(1, NX):
        f = jnp.exp2(tops[d - 1] - top)
        o = o + jnp.where(x >= d, OB[d].astype(F32), 0.0) * f
        l = l + jnp.where(x >= d, SB[d, 1:2, :], 0.0) * f
    attended = (o / l).astype(BF)

    PK[...] = nt(disp, attended).astype(BF).reshape(NZ, ACAP, HEAD)
    acps = [cop.send(PK.at[wrap(z + k, NZ)], ER.at[z], a_s.at[k], a_r.at[k], zdev(k)) for k in range(1, NZ)]
    ER[z] = PK[z]
    wf.wait(1, 3, 4)
    to_sibling(far)
    for cp in wz.values():
        cp.wait_recv()
    to_sibling(wrap(x - 1, NX), wrap(x + 1, NX))
    forward_weights((0,))
    send_weights((1, 2))
    for cp in acps:
        cp.wait_recv()
    lhs = jnp.concatenate([ER[h] for h in range(NZ)], axis=1)
    order = [x, far, wrap(x - 1, NX), wrap(x + 1, NX)]
    real = [part(512, b) for b in order]
    ends = {}

    def project(n):
        wcs[n].wait_recv()
        r = nt(lhs, WO[order[n]].reshape(512, 1024))
        PR[z, :, n * 512:(n + 1) * 512] = r[0:32].astype(BF)
        ends[n] = r[32:40]
        if n % 2 == 1:
            k = n // 2
            PT[z, :, k * 512:(k + 1) * 512] = jnp.concatenate([ends[n - 1], ends[n]], axis=0).astype(BF)
            pring.start(2 * k, 2 * k + 1)

    def wide(slot, k):
        h = (k // 2) * 1024
        return PR.at[slot, :, h:h + 1024] if k % 2 == 0 else PT.at[slot, :, h // 2:h // 2 + 512]

    pring = Rounds(cop, wide, z, zdev, p_s, p_r, 4)
    A, B = (0, 1), (2, 3)
    project(0)
    project(1)
    project(2)
    wait_local(7, 8)
    tables = [nn(sel, MG[i]).astype(BF) for i in range(4)]
    picked = [nn(sel, RB[:, real[n]]) for n in range(4)]
    pring.forward(*A)
    project(3)
    pring.forward(*B)

    def projected(n):
        t = (n // 2) * 512
        return jnp.concatenate(
            [
                PR[:, :, n * 512:(n + 1) * 512].reshape(256, 512),
                PT[:, :, t:t + 512].reshape(128, 512),
            ],
            axis=0,
        )

    xring = Rounds(
        cop, lambda slot, k: XN.at[slot, :, k * 512:(k + 1) * 512], y, ydev, x_s, x_r, 4
    )

    def pick(group):
        pring.wait(*group)
        for n in group:
            rows = projected(n)
            h = 2 * (n % 2)
            XN[y, :, n * 512:(n + 1) * 512] = (
                picked[n] + nn(tables[h], rows) + nn(tables[h + 1], rows)
            ).astype(BF)
            xring.start(n)

    pick(A)
    pick(B)
    xring.forward(*A)

    def normalise(slot):
        v = XN[slot].astype(F32)
        scale = lax.rsqrt(jnp.mean(v * v, axis=1, keepdims=True) + 1e-6)
        for n in range(4):
            XR[slot, :, real[n]] = (v[:, n * 512:(n + 1) * 512] * scale * GN[:, real[n]]).astype(BF)

    near_to_sibling((0,))
    forward_weights((1, 2))
    near_to_sibling((1, 2))
    normalise(y)
    xring.forward(*B)
    for n in range(4):
        rows = projected(n)
        h = 2 * (n % 2)
        RES[:, real[n]] = RB[:, real[n]].astype(F32) + nn(MG[h], rows) + nn(MG[h + 1], rows)
    far_to_sibling((0, 1))
    xring.wait(*A, *B)
    for slot in pair(1) + pair(2) + pair(3) + [wrap(y + 4, NY)]:
        normalise(slot)
    wait_local(10, 11, 12)
    for cp in fcs:
        cp.wait_recv()
    fcs.clear()
    far_to_sibling((2,))
    rows = XR[...].reshape(NY * FCAP, D)
    hidden = []
    for n in (0, 256, 512):
        size = min(256, 704 - n)
        g = nt(rows, W[0].reshape(704, D)[n:n + size])
        u = nt(rows, W[1].reshape(704, D)[n:n + size])
        hidden.append((g / (1.0 + jnp.exp(-g)) * u).astype(BF))
    hidden = jnp.concatenate(hidden, axis=1)
    for cp in fcs:
        cp.wait_recv()

    def cut(ref, k, n):
        return ref.at[k, :, n * 512:(n + 1) * 512]

    hop = {}

    def pass_on(way, near, n, dest, k):
        sign = 1 if way == 0 else -1
        hop[way, near, n] = cop.send(
            cut(YP, wrap(y + sign * dest, NY), n), cut((RR, RL)[way], near, n),
            y_s.at[way, near, n], y_r.at[way, near, n], ydev(sign * k),
        )

    for n in range(4):
        cols = slice(n * 512, (n + 1) * 512)
        YP[:, :, cols] = nn(hidden, W[2, :, :, cols].reshape(704, 512)).astype(BF).reshape(NY, FCAP, 512)
        pass_on(n // 2, 3, n, 4, 2)
        for way in (0, 1):
            pass_on(way, 2, n, 3, 1)
    for n in range(4):
        cols = slice(n * 512, (n + 1) * 512)
        for way in (0, 1):
            got = (RR, RL)[way]
            dest = wrap(y + 2 if way == 0 else y - 2, NY)
            hop[way, 2, n].wait_recv()
            share = YP[dest, :, cols].astype(F32) + got[2, :, cols].astype(F32)
            if way == n // 2:
                hop[way, 3, n].wait_recv()
                share = share + got[3, :, cols].astype(F32)
            YP[dest, :, cols] = share.astype(BF)
            pass_on(way, 1, n, 2, 2)
        for way in (0, 1):
            pass_on(way, 0, n, 1, 1)
    ering = Rounds(
        cop, lambda slot, k: EO.at[slot, :, k * 512:(k + 1) * 512], z, zdev, e_s, e_r, 4
    )
    for n in range(4):
        cols = slice(n * 512, (n + 1) * 512)
        total = YP[y, :, cols].astype(F32)
        for way in (0, 1):
            for near in (0, 1):
                hop[way, near, n].wait_recv()
                total = total + (RR, RL)[way][near, :, cols].astype(F32)
        EO[z, :, cols] = total.astype(BF)
        ering.start(n)
    older = [cp for cp in cop.sent if cp not in ering.cps.values()]
    for cp in older:
        cp.wait_send()
    ering.forward(*A, *B)
    for n in range(4):
        cols = slice(n * 512, (n + 1) * 512)
        ering.wait(n)
        e = EO[:, :, cols].reshape(NZ * FCAP, 512)
        out[:, cols] = (RES[:, cols] + nn(FG[0], e) + nn(FG[1], e)).astype(BF)

    cop.drain()


def shards(
    residual, queries, keys, values, attn_routes, attn_gates, out_weight, norm_gain,
    ffn_routes, ffn_gates, w_gate, w_up, w_down,
):
    hbm = pl.BlockSpec(memory_space=pl.ANY)
    dma = lambda *s: pltpu.SemaphoreType.DMA(s)
    vb = lambda *s: pltpu.VMEM(s, BF)
    vf = lambda *s: pltpu.VMEM(s, F32)
    vi = lambda *s: pltpu.VMEM(s, jnp.int32)
    out = pl.pallas_call(
        layer_kernel,
        name="layer",
        out_shape=jax.ShapeDtypeStruct((TOK, D), BF),
        in_specs=[hbm] * 13,
        out_specs=pl.BlockSpec(memory_space=pltpu.VMEM),
        scratch_shapes=[
            vb(TOK, D),
            vb(2 * TOK, HEAD),
            vi(2, TOK), vf(2, TOK), vi(2, TOK), vf(2, TOK),
            vf(1, D),
            vb(NY, 2, TOK, HEAD),
            vb(NX, 2 * TOK, HEAD),
            vf(NX, HEAD, 2 * TOK),
            vf(NX, 8, 2 * TOK),
            vb(NX, HEAD, 2 * TOK),
            vf(NX, 8, 2 * TOK),
            vb(NX, HEAD, 2 * TOK),
            vf(NX, 8, 2 * TOK),
            vb(NX, NY, 64, 1024),
            vb(3, NX, 176, D),
            vb(NZ, ACAP, HEAD),
            vb(NZ, ACAP, HEAD),
            vb(NZ, 32, D),
            vb(NZ, 16, 1024),
            vb(4, TOK, 384),
            vb(2, TOK, NZ * FCAP),
            vb(NY, FCAP, D),
            vb(NY, FCAP, D),
            vb(NY, FCAP, D),
            vb(4, FCAP, D),
            vb(4, FCAP, D),
            vb(NZ, FCAP, D),
            vf(TOK, D),
            dma(13),
            dma(2, 4), dma(2, 4),
            dma(NX), dma(NX),
            dma(NX, 2), dma(NX, 2),
            dma(2, 4), dma(2, 4),
            dma(2, 4), dma(2, 4),
            dma(2, 2, 8), dma(2, 2, 8),
            dma(4), dma(4),
            dma(2, 3, 2), dma(2, 3, 2),
            dma(2, 3), dma(2, 3),
            dma(3, 3), dma(3, 3),
            dma(8), dma(8),
            dma(2, 4, 4), dma(2, 4, 4),
            dma(2, 4, 4), dma(2, 4, 4),
            dma(2, 4, 4), dma(2, 4, 4),
            dma(2, 4, 4), dma(2, 4, 4),
        ],
        compiler_params=pltpu.CompilerParams(
            collective_id=0, has_side_effects=True, vmem_limit_bytes=56 * 1024 * 1024
        ),
    )(
        residual[0], queries[0].reshape(2 * TOK, HEAD), keys[0], values[0],
        attn_routes[0].T, attn_gates[0].T, ffn_routes[0].T, ffn_gates[0].T,
        norm_gain.reshape(1, D), out_weight[0].T, w_gate[0].T, w_up[0].T, w_down[0],
    )
    return out[None]


def solution(mesh):
    in_specs = (
        P("dp", "ctx", None),
        P("dp", "ctx", None, "exp"),
        P("dp", "ctx", "exp"),
        P("dp", "ctx", "exp"),
        P("dp", "ctx", None),
        P("dp", "ctx", None),
        P("exp", None, "ctx"),
        P(),
        P("dp", "ctx", None),
        P("dp", "ctx", None),
        P("exp", None, "ctx"),
        P("exp", None, "ctx"),
        P("exp", "ctx", None),
    )
    out_specs = P("dp", "ctx", None)
    return jax.shard_map(shards, mesh=mesh, in_specs=in_specs, out_specs=out_specs, check_vma=False)
```

```python
import functools
import math

import jax
import jax.numpy as jnp
from jax import lax
from jax.experimental import pallas as pl
from jax.experimental.pallas import tpu as pltpu
from jax.sharding import PartitionSpec as P

MESH = pl.DeviceIdType.MESH
BF = jnp.bfloat16
F32 = jnp.float32
NX, NY, NZ = 4, 8, 8
TOK = 128
D = 2048
HEAD = 128
ACAP = 48
FCAP = 32
NEG = -1e30


def nt(a, b):
    return lax.dot_general(a, b, (((1,), (1,)), ((), ())), preferred_element_type=F32)


def tn(a, b):
    return lax.dot_general(a, b, (((0,), (0,)), ((), ())), preferred_element_type=F32)


def nn(a, b):
    return jnp.dot(a, b, preferred_element_type=F32)


def wrap(v, n):
    return lax.rem(v + 2 * n, n)


class Copy:
    def __init__(self, src, dst, ssem, rsem, dev, sends=None, gets=None):
        self.cp = pltpu.make_async_remote_copy(
            src_ref=src, dst_ref=dst, send_sem=ssem, recv_sem=rsem, device_id=dev, device_id_type=MESH
        )
        self.sends, self.gets = sends, gets
        self.done = self.left = False

    def _when(self, cond, act):
        if cond is None:
            act()
        else:
            pl.when(cond)(act)

    def start(self):
        self._when(self.sends, self.cp.start)

    def wait_recv(self):
        self.done = True
        self._when(self.gets, self.cp.wait_recv)

    def wait_send(self):
        if not self.left:
            self.left = True
            self._when(self.sends, self.cp.wait_send)


class Copies:
    def __init__(self):
        self.sent = []

    def send(self, src, dst, ssem, rsem, dev, sends=None, gets=None):
        cp = Copy(src, dst, ssem, rsem, dev, sends, gets)
        cp.start()
        self.sent.append(cp)
        return cp

    def drain(self):
        for cp in self.sent:
            if not cp.done:
                cp.wait_recv()
        self.flush()

    def flush(self):
        for cp in self.sent:
            cp.wait_send()
        self.sent = [cp for cp in self.sent if not cp.done]


class Ring:
    def __init__(self, copies, at, pos, right, left, ssem, rsem, chunks):
        self.copies, self.at, self.pos = copies, at, pos
        self.devs = (right, left)
        self.ssem, self.rsem, self.chunks = ssem, rsem, chunks
        self.cps = {}

    def carries(self, way, step, j):
        return step < 4 or (j < self.chunks // 2) == (way == 0)

    def slot(self, way, step):
        return wrap(self.pos - step if way == 0 else self.pos + step, 8)

    def start(self, step, j):
        for way in (0, 1):
            if self.carries(way, step, j):
                slot = self.slot(way, step - 1)
                src = self.at(slot, j)
                self.cps[way, step, j] = self.copies.send(
                    src, self.at(slot, j), self.ssem.at[way, step - 1, j], self.rsem.at[way, step - 1, j], self.devs[way]
                )

    def wait(self, step, j):
        for way in (0, 1):
            if self.carries(way, step, j):
                self.cps[way, step, j].wait_recv()

    def forward(self, step, js=None):
        for j in range(self.chunks) if js is None else js:
            if step > 1:
                self.wait(step - 1, j)
            self.start(step, j)

    def finish(self):
        for j in range(self.chunks):
            self.wait(4, j)


class Two:
    def __init__(self, copies, at, pos, dev, ssem, rsem, own=None):
        self.copies, self.at, self.pos, self.dev = copies, at, pos, dev
        self.ssem, self.rsem, self.own = ssem, rsem, own
        self.cps = {}

    def _send(self, way, n, ref, k, src=None):
        sign = 1 if way == 0 else -1
        self.cps[way, n] = self.copies.send(
            ref if src is None else src, ref, self.ssem.at[way, n - 1], self.rsem.at[way, n - 1], self.dev(sign * k)
        )

    def start(self):
        for k in (2, 1):
            for way in (0, 1):
                self._send(way, k, self.at(self.pos, None), k, self.own)

    def forward(self):
        for way in (0, 1):
            self.cps[way, 2].wait_recv()
        for way in (0, 1):
            slot = wrap(self.pos - 2 if way == 0 else self.pos + 2, 8)
            self._send(way, 4, self.at(slot, way), 2)
            self._send(way, 3, self.at(slot, None), 1)

    def wait(self, *ns):
        for n in ns:
            for way in (0, 1):
                self.cps[way, n].wait_recv()


class Rounds:
    def __init__(self, copies, at, pos, dev, ssem, rsem, chunks):
        self.copies, self.at, self.pos, self.dev = copies, at, pos, dev
        self.ssem, self.rsem, self.chunks = ssem, rsem, chunks
        self.cps = {}

    def _send(self, way, n, j, slot, k):
        ref = self.at(slot, j)
        self.cps[way, n, j] = self.copies.send(
            ref, ref, self.ssem.at[way, n - 1, j], self.rsem.at[way, n - 1, j],
            self.dev(k if way == 0 else -k),
        )

    def start(self, *js):
        for j in js:
            for k in (2, 1):
                for way in (0, 1):
                    self._send(way, k, j, self.pos, k)

    def forward(self, *js):
        for j in js:
            for way in (0, 1):
                self.cps[way, 2, j].wait_recv()
                slot = wrap(self.pos - 2 if way == 0 else self.pos + 2, 8)
                if (j < self.chunks // 2) == (way == 0):
                    self._send(way, 4, j, slot, 2)
                self._send(way, 3, j, slot, 1)

    def wait(self, *js):
        for j in js:
            for n in (1, 3, 4):
                for way in (0, 1):
                    if (way, n, j) in self.cps:
                        self.cps[way, n, j].wait_recv()


def layer_kernel(
    res, q, kk, vv, ar, ag, fr, fg, gain, wo, wg, wu, wd, out,
    RB, QV, AR, AG, FR, FGT, GN, KV, QB, OA, ML, OB, SB, OS, SS, WO, W, PK, ER, PR, PT, MG, FG, XN, XR, YP, RR, RL,
    EO, RES,
    l_s, kv_s, kv_r, q_s, q_r, o_s, o_r, wb_s, wb_r, wy_s, wy_r, wz_s, wz_r, wc_s, wc_r,
    fx_s, fx_r, fa_s, fa_r, fc_s, fc_r, a_s, a_r, p_s, p_r, x_s, x_r, y_s, y_r, e_s, e_r,
):
    j = lax.axis_index("dp")
    c = lax.axis_index("ctx")
    z = lax.axis_index("exp")
    x = c // NY
    y = c % NY
    cop = Copies()

    def xdev(k):
        return (j, wrap(x + k, NX) * NY + y, z)

    def ydev(k):
        return (j, x * NY + wrap(y + k, NY), z)

    def zdev(k):
        return (j, c, wrap(z + k, NZ))

    sib = (1 - j, c, z)

    def part(n, i):
        return pl.ds(pl.multiple_of(i * n, n), n)

    barrier = pltpu.get_barrier_semaphore()
    partners = [xdev(k) for k in (1, 2, 3)] + [ydev(k) for k in (1, 2, -2, -1)] + [zdev(k) for k in range(1, 8)] + [sib]
    for dev in partners:
        pl.semaphore_signal(barrier, inc=1, device_id=dev, device_id_type=MESH)

    local = [
        (kk, KV.at[y, 0]), (vv, KV.at[y, 1]), (q, QV),
        (ar, AR), (ag, AG), (fr, FR), (fg, FGT),
        (res, RB), (gain, GN),
        (wo.at[:, part(512, j)], WO.at[x, y, :, part(512, j)]),
        (wg, W.at[0, x]), (wu, W.at[1, x]), (wd, W.at[2, x]),
    ]
    own_w = [pltpu.make_async_copy(src, dst, l_s.at[i]) for i, (src, dst) in enumerate(local)]

    def wait_local(*ids):
        for i in ids:
            own_w[i].wait()

    for cp in own_w:
        cp.start()
    pl.semaphore_wait(barrier, len(partners))

    lanes = part(512, j)
    def held(i):
        return lambda slot, h: KV.at[slot, i] if h is None else KV.at[slot, i, 64 * h:64 * h + 64]

    kvrings = [
        Two(cop, held(i), y, ydev, kv_s.at[i], kv_r.at[i], own) for i, own in enumerate((kk, vv))
    ]
    for ring in kvrings:
        ring.start()
    qcp = {
        d: cop.send(q, QB.at[d], q_s.at[d], q_r.at[d], xdev(-d), sends=x >= d, gets=x + d < NX)
        for d in (3, 2, 1)
    }

    def block(slot, h):
        if h is None:
            return WO.at[x, slot, :, lanes]
        return WO.at[x, slot, 32 * h:32 * h + 32, lanes]

    far = wrap(x + 2, NX)

    def far_block(slot, h):
        if h is None:
            return WO.at[far, slot, :, lanes]
        return WO.at[far, slot, 32 * h:32 * h + 32, lanes]

    wb = Two(cop, block, y, ydev, wb_s, wb_r)
    wf = Two(cop, far_block, y, ydev, wy_s, wy_r)
    wz = {}
    wcs = []

    def to_sibling(*slots):
        for slot in slots:
            n = len(wcs)
            ref = WO.at[slot, :, :, lanes]
            wcs.append(cop.send(ref, ref, wc_s.at[n], wc_r.at[n], sib))

    def along_x(*ns):
        for n in ns:
            slot = wrap(y + n, NY)
            for way, step in ((0, 1), (1, -1)):
                wz[way, 0, n] = cop.send(
                    wo.at[:, lanes] if n == 0 else WO.at[x, slot, :, lanes], WO.at[x, slot, :, lanes],
                    wz_s.at[way, 0, n], wz_r.at[way, 0, n], xdev(step),
                )

    along_x(0)
    across = cop.send(wo.at[:, lanes], WO.at[x, y, :, lanes], wz_s.at[0, 1, 0], wz_r.at[0, 1, 0], xdev(2))

    quarter = [pl.ds(pl.multiple_of(j * 1024 + h * 512, 512), 512) for h in (0, 1)]
    fx = {}

    def send_weights(which):
        for turn in (0, 1):
            for way, step in ((0, 1), (1, -1)):
                h = turn if way == 0 else 1 - turn
                for i in which:
                    fx[way, i, h] = cop.send(
                        (wg, wu, wd)[i].at[:, quarter[h]], W.at[i, x, :, quarter[h]],
                        fx_s.at[way, i, h], fx_r.at[way, i, h], xdev(step),
                    )

    fa = {}

    def forward_weights(which):
        for way, step in ((0, 1), (1, -1)):
            slot = wrap(x - step, NX)
            for i in which:
                fx[way, i, way].wait_recv()
                ref = W.at[i, slot, :, quarter[way]]
                fa[way, i] = cop.send(ref, ref, fa_s.at[way, i], fa_r.at[way, i], xdev(step))

    fcs = []

    def weights_to_sibling(n, which, slot):
        for i in which:
            ref = W.at[i, slot, :, part(1024, j)]
            fcs.append(cop.send(ref, ref, fc_s.at[n, i], fc_r.at[n, i], sib))

    def near_to_sibling(which):
        for way, step in ((0, 1), (1, -1)):
            for i in which:
                fx[way, i, 1 - way].wait_recv()
            weights_to_sibling(way, which, wrap(x - step, NX))

    def far_to_sibling(which):
        for i in which:
            for way in (0, 1):
                fa[way, i].wait_recv()
        weights_to_sibling(2, which, wrap(x + 2, NX))

    send_weights((0,))

    factor = math.log2(math.e) / math.sqrt(HEAD)

    def absorb(d, blocks, first=False, last=False):
        queries = QV[...] if d == 0 else QB[d]
        ks = jnp.concatenate([KV[b, 0] for b in blocks], axis=0)
        vs = jnp.concatenate([KV[b, 1] for b in blocks], axis=0)
        s = nt(ks, queries) * factor
        if d == 0:
            row = lax.broadcasted_iota(jnp.int32, (TOK, 2 * TOK), 0)
            qpos = y * TOK + lax.shift_right_logical(
                lax.broadcasted_iota(jnp.int32, (TOK, 2 * TOK), 1), 1
            )
            allowed = jnp.concatenate([row + b * TOK - qpos for b in blocks], axis=0) <= 0
            s = jnp.where(allowed, s, NEG)
        m = jnp.max(s, axis=0, keepdims=True)
        if not first:
            old = ML[d, 0:1, :]
            m = jnp.maximum(m, old)
        p = jnp.exp2(s - m)
        l = jnp.sum(p, axis=0, keepdims=True)
        o = tn(vs, p.astype(BF))
        if not first:
            shrink = jnp.exp2(old - m)
            l = l + ML[d, 1:2, :] * shrink
            o = o + OA[d] * shrink
        if last:
            return o, m, l
        ML[d, 0:1, :] = m
        ML[d, 1:2, :] = l
        OA[d] = o

    def absorb_later(blocks, first=False):
        for d in range(1, NX):

            @pl.when(x + d < NX)
            def _():
                absorb(d, blocks, first)

    def pair(step):
        return [wrap(y - step, NY), wrap(y + step, NY)]

    wait_local(0, 1, 2, 9)
    absorb(0, [y], first=True)
    wb.start()

    wait_local(3, 4, 5, 6)
    upper = (
        lax.broadcasted_iota(jnp.int32, (256, 256), 0) < lax.broadcasted_iota(jnp.int32, (256, 256), 1)
    ).astype(F32).astype(BF)

    def ranks(route):
        eid = lax.broadcasted_iota(jnp.int32, (8, 256), 0).astype(F32)
        onehot = (eid == route).astype(F32)
        before = nn(onehot.astype(BF), upper)
        return jnp.sum(before * onehot, axis=0, keepdims=True)

    def iota0(rows, cols):
        return lax.broadcasted_iota(jnp.int32, (rows, cols), 0).astype(F32)

    def gate_table(slot, gates, rows):
        rid = iota0(rows, TOK)
        t = jnp.where(rid == slot[:, :TOK], gates[0:1, :], 0.0) + jnp.where(
            rid == slot[:, TOK:], gates[1:2, :], 0.0
        )
        t = t.T
        hi = t.astype(BF)
        return hi, (t - hi.astype(F32)).astype(BF)

    aroute = AR[...].astype(F32)
    aroute = jnp.concatenate([aroute[0:1, :], aroute[1:2, :]], axis=1)
    arank = ranks(aroute)
    by_slot = (iota0(8 * ACAP, 256) == aroute * ACAP + arank).astype(F32).astype(BF)
    src = lax.broadcasted_iota(jnp.int32, (256, 256), 0)
    dst = 2 * jnp.bitwise_and(src, TOK - 1) + lax.shift_right_logical(src, 7)
    swap = (lax.broadcasted_iota(jnp.int32, (256, 256), 1) == dst).astype(F32).astype(BF)
    disp = nn(by_slot, swap).astype(BF)
    main = aroute * 32 + arank
    extra = 256 + aroute * 16 + (arank - 32)
    agates = AG[...]
    for i in range(2):
        MG[2 * i], MG[2 * i + 1] = gate_table(jnp.where(arank < 32, main, extra + 8 * i), agates, 384)

    froute = FR[...].astype(F32)
    froute = jnp.concatenate([froute[0:1, :], froute[1:2, :]], axis=1)
    fslot = froute * FCAP + ranks(froute)
    FG[0], FG[1] = gate_table(fslot, FGT[...], 8 * FCAP)
    mine = iota0(FCAP, TOK) + (z * FCAP).astype(F32)
    sel = ((mine == fslot[:, :TOK]).astype(F32) + (mine == fslot[:, TOK:]).astype(F32)).astype(BF)

    for ring in kvrings:
        ring.forward()
    for ring in kvrings:
        ring.wait(1)
    near = pair(1) + pair(2)
    absorb(0, near)
    for d in range(1, NX):
        qcp[d].wait_recv()
    absorb_later([y] + near, first=True)
    wb.forward()
    wb.wait(1)
    along_x(1, 7, 2, 6)
    for ring in kvrings:
        ring.wait(3, 4)
    across.wait_recv()
    wf.start()
    ocp = []
    final = pair(3) + [wrap(y + 4, NY)]
    for d in (3, 2, 1):

        @pl.when(x + d < NX)
        def _():
            o, m, l = absorb(d, final, last=True)
            OS[d] = o.astype(BF)
            SS[d] = jnp.concatenate([m, l, jnp.zeros((6, 2 * TOK), F32)], axis=0)

        for src, dst, i in ((OS, OB, 0), (SS, SB, 1)):
            ocp.append(
                cop.send(
                    src.at[d], dst.at[d], o_s.at[d, i], o_r.at[d, i], xdev(d),
                    sends=x + d < NX, gets=x >= d,
                )
            )
    o, m, l = absorb(0, final, last=True)
    wb.wait(3, 4)
    along_x(3, 5, 4)
    to_sibling(x)
    wf.forward()
    for cp in ocp:
        cp.wait_recv()
    tops = [jnp.where(x >= d, SB[d, 0:1, :], NEG) for d in range(1, NX)]
    top = m
    for t in tops:
        top = jnp.maximum(top, t)
    f = jnp.exp2(m - top)
    o = o * f
    l = l * f
    for d in range(1, NX):
        f = jnp.exp2(tops[d - 1] - top)
        o = o + jnp.where(x >= d, OB[d].astype(F32), 0.0) * f
        l = l + jnp.where(x >= d, SB[d, 1:2, :], 0.0) * f
    attended = (o / l).astype(BF)

    PK[...] = nt(disp, attended).astype(BF).reshape(NZ, ACAP, HEAD)
    acps = [cop.send(PK.at[wrap(z + k, NZ)], ER.at[z], a_s.at[k], a_r.at[k], zdev(k)) for k in range(1, NZ)]
    ER[z] = PK[z]
    wf.wait(1, 3, 4)
    to_sibling(far)
    for cp in wz.values():
        cp.wait_recv()
    to_sibling(wrap(x - 1, NX), wrap(x + 1, NX))
    forward_weights((0,))
    send_weights((1, 2))
    for cp in acps:
        cp.wait_recv()
    lhs = jnp.concatenate([ER[h] for h in range(NZ)], axis=1)
    order = [x, far, wrap(x - 1, NX), wrap(x + 1, NX)]
    real = [part(512, b) for b in order]
    ends = {}

    def project(n):
        wcs[n].wait_recv()
        r = nt(lhs, WO[order[n]].reshape(512, 1024))
        PR[z, :, n * 512:(n + 1) * 512] = r[0:32].astype(BF)
        ends[n] = r[32:40]
        if n % 2 == 1:
            k = n // 2
            PT[z, :, k * 512:(k + 1) * 512] = jnp.concatenate([ends[n - 1], ends[n]], axis=0).astype(BF)
            pring.start(2 * k, 2 * k + 1)

    def wide(slot, k):
        h = (k // 2) * 1024
        return PR.at[slot, :, h:h + 1024] if k % 2 == 0 else PT.at[slot, :, h // 2:h // 2 + 512]

    pring = Rounds(cop, wide, z, zdev, p_s, p_r, 4)
    A, B = (0, 1), (2, 3)
    project(0)
    project(1)
    project(2)
    wait_local(7, 8)
    tables = [nn(sel, MG[i]).astype(BF) for i in range(4)]
    picked = [nn(sel, RB[:, real[n]]) for n in range(4)]
    pring.forward(*A)
    project(3)
    pring.forward(*B)

    def projected(n):
        t = (n // 2) * 512
        return jnp.concatenate(
            [
                PR[:, :, n * 512:(n + 1) * 512].reshape(256, 512),
                PT[:, :, t:t + 512].reshape(128, 512),
            ],
            axis=0,
        )

    xring = Rounds(
        cop, lambda slot, k: XN.at[slot, :, k * 512:(k + 1) * 512], y, ydev, x_s, x_r, 4
    )

    def pick(group):
        pring.wait(*group)
        for n in group:
            rows = projected(n)
            h = 2 * (n % 2)
            XN[y, :, n * 512:(n + 1) * 512] = (
                picked[n] + nn(tables[h], rows) + nn(tables[h + 1], rows)
            ).astype(BF)
            xring.start(n)

    pick(A)
    pick(B)
    xring.forward(*A)

    def normalise(slot):
        v = XN[slot].astype(F32)
        scale = lax.rsqrt(jnp.mean(v * v, axis=1, keepdims=True) + 1e-6)
        for n in range(4):
            XR[slot, :, real[n]] = (v[:, n * 512:(n + 1) * 512] * scale * GN[:, real[n]]).astype(BF)

    near_to_sibling((0,))
    forward_weights((1, 2))
    near_to_sibling((1, 2))
    normalise(y)
    xring.forward(*B)
    for n in range(4):
        rows = projected(n)
        h = 2 * (n % 2)
        RES[:, real[n]] = RB[:, real[n]].astype(F32) + nn(MG[h], rows) + nn(MG[h + 1], rows)
    far_to_sibling((0, 1))
    xring.wait(*A, *B)
    for slot in pair(1) + pair(2) + pair(3) + [wrap(y + 4, NY)]:
        normalise(slot)
    wait_local(10, 11, 12)
    for cp in fcs:
        cp.wait_recv()
    fcs.clear()
    far_to_sibling((2,))
    rows = XR[...].reshape(NY * FCAP, D)
    hidden = []
    for n in (0, 256, 512):
        size = min(256, 704 - n)
        g = nt(rows, W[0].reshape(704, D)[n:n + size])
        u = nt(rows, W[1].reshape(704, D)[n:n + size])
        hidden.append((g / (1.0 + jnp.exp(-g)) * u).astype(BF))
    hidden = jnp.concatenate(hidden, axis=1)
    for cp in fcs:
        cp.wait_recv()

    def cut(ref, k, n):
        return ref.at[k, :, n * 512:(n + 1) * 512]

    hop = {}

    def pass_on(way, near, n, dest, k):
        sign = 1 if way == 0 else -1
        hop[way, near, n] = cop.send(
            cut(YP, wrap(y + sign * dest, NY), n), cut((RR, RL)[way], near, n),
            y_s.at[way, near, n], y_r.at[way, near, n], ydev(sign * k),
        )

    for n in range(4):
        cols = slice(n * 512, (n + 1) * 512)
        YP[:, :, cols] = nn(hidden, W[2, :, :, cols].reshape(704, 512)).astype(BF).reshape(NY, FCAP, 512)
        pass_on(n // 2, 3, n, 4, 2)
        for way in (0, 1):
            pass_on(way, 2, n, 3, 1)
    for n in range(4):
        cols = slice(n * 512, (n + 1) * 512)
        for way in (0, 1):
            got = (RR, RL)[way]
            dest = wrap(y + 2 if way == 0 else y - 2, NY)
            hop[way, 2, n].wait_recv()
            share = YP[dest, :, cols].astype(F32) + got[2, :, cols].astype(F32)
            if way == n // 2:
                hop[way, 3, n].wait_recv()
                share = share + got[3, :, cols].astype(F32)
            YP[dest, :, cols] = share.astype(BF)
            pass_on(way, 1, n, 2, 2)
        for way in (0, 1):
            pass_on(way, 0, n, 1, 1)
    ering = Rounds(
        cop, lambda slot, k: EO.at[slot, :, k * 512:(k + 1) * 512], z, zdev, e_s, e_r, 4
    )
    for n in range(4):
        cols = slice(n * 512, (n + 1) * 512)
        total = YP[y, :, cols].astype(F32)
        for way in (0, 1):
            for near in (0, 1):
                hop[way, near, n].wait_recv()
                total = total + (RR, RL)[way][near, :, cols].astype(F32)
        EO[z, :, cols] = total.astype(BF)
        ering.start(n)
    older = [cp for cp in cop.sent if cp not in ering.cps.values()]
    for cp in older:
        cp.wait_send()
    ering.forward(*A, *B)
    for n in range(4):
        cols = slice(n * 512, (n + 1) * 512)
        ering.wait(n)
        e = EO[:, :, cols].reshape(NZ * FCAP, 512)
        out[:, cols] = (RES[:, cols] + nn(FG[0], e) + nn(FG[1], e)).astype(BF)

    cop.drain()


def shards(
    residual, queries, keys, values, attn_routes, attn_gates, out_weight, norm_gain,
    ffn_routes, ffn_gates, w_gate, w_up, w_down,
):
    hbm = pl.BlockSpec(memory_space=pl.ANY)
    dma = lambda *s: pltpu.SemaphoreType.DMA(s)
    vb = lambda *s: pltpu.VMEM(s, BF)
    vf = lambda *s: pltpu.VMEM(s, F32)
    vi = lambda *s: pltpu.VMEM(s, jnp.int32)
    out = pl.pallas_call(
        layer_kernel,
        name="layer",
        out_shape=jax.ShapeDtypeStruct((TOK, D), BF),
        in_specs=[hbm] * 13,
        out_specs=pl.BlockSpec(memory_space=pltpu.VMEM),
        scratch_shapes=[
            vb(TOK, D),
            vb(2 * TOK, HEAD),
            vi(2, TOK), vf(2, TOK), vi(2, TOK), vf(2, TOK),
            vf(1, D),
            vb(NY, 2, TOK, HEAD),
            vb(NX, 2 * TOK, HEAD),
            vf(NX, HEAD, 2 * TOK),
            vf(NX, 8, 2 * TOK),
            vb(NX, HEAD, 2 * TOK),
            vf(NX, 8, 2 * TOK),
            vb(NX, HEAD, 2 * TOK),
            vf(NX, 8, 2 * TOK),
            vb(NX, NY, 64, 1024),
            vb(3, NX, 176, D),
            vb(NZ, ACAP, HEAD),
            vb(NZ, ACAP, HEAD),
            vb(NZ, 32, D),
            vb(NZ, 16, 1024),
            vb(4, TOK, 384),
            vb(2, TOK, NZ * FCAP),
            vb(NY, FCAP, D),
            vb(NY, FCAP, D),
            vb(NY, FCAP, D),
            vb(4, FCAP, D),
            vb(4, FCAP, D),
            vb(NZ, FCAP, D),
            vf(TOK, D),
            dma(13),
            dma(2, 2, 4), dma(2, 2, 4),
            dma(NX), dma(NX),
            dma(NX, 2), dma(NX, 2),
            dma(2, 4), dma(2, 4),
            dma(2, 4), dma(2, 4),
            dma(2, 2, 8), dma(2, 2, 8),
            dma(4), dma(4),
            dma(2, 3, 2), dma(2, 3, 2),
            dma(2, 3), dma(2, 3),
            dma(3, 3), dma(3, 3),
            dma(8), dma(8),
            dma(2, 4, 4), dma(2, 4, 4),
            dma(2, 4, 4), dma(2, 4, 4),
            dma(2, 4, 4), dma(2, 4, 4),
            dma(2, 4, 4), dma(2, 4, 4),
        ],
        compiler_params=pltpu.CompilerParams(
            collective_id=0, has_side_effects=True, vmem_limit_bytes=56 * 1024 * 1024
        ),
    )(
        residual[0], queries[0].reshape(2 * TOK, HEAD), keys[0], values[0],
        attn_routes[0].T, attn_gates[0].T, ffn_routes[0].T, ffn_gates[0].T,
        norm_gain.reshape(1, D), out_weight[0].T, w_gate[0].T, w_up[0].T, w_down[0],
    )
    return out[None]


def solution(mesh):
    in_specs = (
        P("dp", "ctx", None),
        P("dp", "ctx", None, "exp"),
        P("dp", "ctx", "exp"),
        P("dp", "ctx", "exp"),
        P("dp", "ctx", None),
        P("dp", "ctx", None),
        P("exp", None, "ctx"),
        P(),
        P("dp", "ctx", None),
        P("dp", "ctx", None),
        P("exp", None, "ctx"),
        P("exp", None, "ctx"),
        P("exp", "ctx", None),
    )
    out_specs = P("dp", "ctx", None)
    return jax.shard_map(shards, mesh=mesh, in_specs=in_specs, out_specs=out_specs, check_vma=False)
```
